256 devices in a mesh: dp: 4 (over x), owner: 64 (over z, y, core).
Axes of the slice: x: 4, y: 4, z: 8, core: 2. Of those that a mesh axis runs over, the one named last changes fastest.
Arguments:
- tokens: bfloat16 [32768, 2048], P(('dp', 'owner')), may hold values from -6 to 6
- grads: bfloat16 [32768, 8, 768], P(('dp', 'owner')), may hold values from -0.19921875 to 0.19921875
- routing: int32 [32768, 8], P(('dp', 'owner')), may hold values from 0 to 127, as said below
- basis_in: bfloat16 [64, 2048, 2048], P('owner'), may hold values from -0.125 to 0.125
- basis_out: bfloat16 [64, 768, 768], P('owner'), may hold values from -0.21875 to 0.21875
Outputs:
- eigenvalues: float32 [2048, 64, 768], P('dp', 'owner')
The draws below stay inside these ranges and needn't reach their ends.
Inputs may be any that keep to these rules, and one draw needn't show every extreme that they name: `routing`: in each device's block of 128 tokens no expert is chosen by more than 16 tokens, and some expert below 64 is chosen by exactly 16 tokens of every block. The 8 experts of one token differ.
All inputs are finite; a program needn't handle non-finite values.
Results may differ from the reference program's by a relative error of at most 0.00048.
Values may be sent and summed in bfloat16 or wider, within the bound.
No kernel may reach another device: no remote copies, remote signals or barrier semaphores. Data moves between devices by JAX's collectives and lax.ppermute only.
A program may use at most 128 MiB of HBM per device.

```python
import jax
import jax.numpy as jnp
from jax import lax

D = 2048
FF = 768
EXPERTS_ALL = 128
TOP = 8
TOK_DEV = 128
EXPERTS = 64
CAP = 16
TOKENS = 32768
N_DP = 4
N_OWNER = 64


def draw_routing(key, part):
    key = jax.random.fold_in(key, 11)
    blocks = TOKENS // TOK_DEV
    classes = EXPERTS_ALL // TOP
    halves = classes // 2
    key_hot, key_split, key_order, key_label = jax.random.split(key, 4)
    hot_expert = jax.random.randint(key_hot, (), 0, EXPERTS)
    split_at = jax.random.randint(key_split, (blocks, halves), 0, CAP + 1)
    split_at = split_at.at[:, 0].set(CAP)
    position = jnp.arange(TOK_DEV)
    which_half = position // CAP
    within = position % CAP
    label = 2 * which_half[None, :] + (within[None, :] >= split_at[:, which_half]).astype(jnp.int32)
    order_keys = jax.random.split(key_order, blocks)
    order = jax.vmap(lambda k: jax.random.permutation(k, TOK_DEV))(order_keys)
    label = jnp.take_along_axis(label, order, axis=1)
    label_keys = jax.random.split(key_label, blocks)
    mixed = jax.vmap(lambda k: jax.random.permutation(k, EXPERTS_ALL))(label_keys)
    relabel = (mixed - mixed[:, :1] + hot_expert) % EXPERTS_ALL
    index = label[:, :, None] + classes * jnp.arange(TOP)[None, None, :]
    chosen = jax.vmap(lambda table, idx: table[idx])(relabel, index)
    return chosen.reshape(TOKENS, TOP).astype(jnp.int32)


def block_scale(own_key, shape, cuts, smallest, high):
    factor_of = 1.0
    for dim, blocks in cuts:
        heights = jax.random.uniform(jax.random.fold_in(jax.random.fold_in(own_key, 6), dim), (blocks,), jnp.float32, smallest / len(cuts), high / len(cuts))
        factor_of = factor_of * jnp.repeat(jnp.exp(heights), shape[dim] // blocks).reshape((-1,) + (1,) * (len(shape) - 1 - dim))
    return factor_of


def normal_values(stream_key, dims, scale, most, shards=(), kind=jnp.bfloat16):
    factor_of = block_scale(stream_key, dims, shards, -0.22, 0.18) if shards else 1.0
    values = jax.random.normal(stream_key, dims, jnp.float32) * scale * factor_of
    return jnp.minimum(jnp.maximum(values, -most), most).astype(kind)


def setup_inputs(seed: int = 0) -> dict:
    seeds = jax.random.split(jax.random.key(seed), 6)
    tokens = normal_values(seeds[0], (TOKENS, D), 1.0, 6.0, ((0, 256),))
    grads = normal_values(seeds[1], (TOKENS, TOP, FF), 0.03, 0.19921875, ((0, 256),))
    routing = draw_routing(jax.random.fold_in(seeds[5], 71), 0)
    basis_in = normal_values(seeds[3], (EXPERTS, D, D), D ** -0.5, 0.125, ((0, 64),))
    basis_out = normal_values(seeds[4], (EXPERTS, FF, FF), FF ** -0.5, 0.21875, ((0, 64),))
    return {"tokens": tokens, "grads": grads, "routing": routing, "basis_in": basis_in, "basis_out": basis_out}


def reference(tokens, grads, routing, basis_in, basis_out):
    blocks = N_DP * N_OWNER
    pairs = TOK_DEV * TOP
    total = blocks * pairs
    flat = routing.reshape(blocks, pairs)
    grad_rows = grads.reshape(total, FF)
    pair_ids = jnp.arange(total, dtype=jnp.int32).reshape(blocks, pairs)
    block_base = (jnp.arange(blocks, dtype=jnp.int32) * CAP)[:, None]

    def one_expert(expert):
        hit = (flat == expert).astype(jnp.int32)
        rank = jnp.cumsum(hit, axis=1) - hit
        slot = jnp.where(hit > 0, block_base + rank, blocks * CAP).astype(jnp.int32)
        chosen = jnp.full((blocks * CAP,), total, jnp.int32)
        chosen = chosen.at[slot.reshape(-1)].set(pair_ids.reshape(-1), mode="drop")
        valid = chosen < total
        safe = jnp.minimum(chosen, total - 1).astype(jnp.int32)
        in_rows = tokens[safe // TOP]
        out_rows = jnp.where(valid[:, None], grad_rows[safe], jnp.zeros((), jnp.bfloat16))
        rotated_in = jnp.dot(in_rows, basis_in[expert], preferred_element_type=jnp.float32)
        a_sq = (rotated_in * rotated_in).astype(jnp.bfloat16)
        rotated_out = jnp.dot(out_rows, basis_out[expert], preferred_element_type=jnp.float32)
        g_sq = (rotated_out * rotated_out).astype(jnp.bfloat16)
        return jnp.dot(a_sq.T, g_sq, preferred_element_type=jnp.float32)

    values = lax.map(one_expert, jnp.arange(EXPERTS, dtype=jnp.int32))
    return jnp.transpose(values, (1, 0, 2))
```

```python
import functools

import jax
import jax.numpy as jnp
from jax import lax
from jax.experimental import pallas as pl
from jax.experimental.pallas import tpu as pltpu
from jax.sharding import Mesh
from jax.sharding import PartitionSpec as P

CAP = 16
N_X, N_Z, N_Y, N_C = 4, 8, 4, 2
N_YC = N_Y * N_C
TURNS = [(0, 0), (0, 1), (1, 0), (1, 1), (3, 0), (3, 1), (2, 0), (2, 1)]
FIRST = (0, 1, 7, 2, 6)
SECOND = (3, 5, 4)
ORDER = FIRST + SECOND
TOK = 128
TOP = 8
D = 2048
WIDE = D // 2
FF = 768
EXPERTS = 64
ROWS = EXPERTS * CAP
QUARTER = D // N_X
HALF = QUARTER // 2
CODE_ROWS = HALF + 16
BF = jnp.bfloat16
F32 = jnp.float32
I32 = jnp.int32
MIB = 1024 * 1024
IN_SMEM = pl.BlockSpec(memory_space=pltpu.SMEM)
IN_VMEM = pl.BlockSpec(memory_space=pltpu.VMEM)


def iota(shape, dim):
    return lax.broadcasted_iota(I32, shape, dim)


def params(mib):
    return pltpu.CompilerParams(vmem_limit_bytes=mib * MIB)


def ones_where(mask):
    return jnp.where(mask, 1.0, 0.0).astype(BF)


def earlier(n):
    return ones_where(iota((n, n), 0) < iota((n, n), 1))


def stage_kernel(tokens_ref, routing_ref, left_ref, right_ref):
    left_ref[0:TOK, :] = tokens_ref[:, 0:WIDE]
    left_ref[TOK:, :] = jnp.zeros((TOP, WIDE), BF)
    left_ref[TOK:, 0:TOK] = routing_ref[...].astype(F32).astype(BF)
    right_ref[...] = tokens_ref[:, WIDE:]


def stage(tokens, routing):
    return pl.pallas_call(
        stage_kernel,
        out_shape=(
            jax.ShapeDtypeStruct((TOK + TOP, WIDE), BF),
            jax.ShapeDtypeStruct((TOK, WIDE), BF),
        ),
        compiler_params=params(8),
    )(tokens, routing)


def pack_grads_kernel(here_ref, flat_ref, grads_ref, *out_refs):
    pairs = TOK * TOP
    flat = flat_ref[...]
    hit = iota((EXPERTS, pairs), 0) == flat
    before = jnp.dot(ones_where(hit), earlier(pairs), preferred_element_type=F32)
    rank = jnp.sum(jnp.where(hit, before, 0.0), axis=0, keepdims=True).astype(I32)
    along_z = (flat // N_YC + N_Z - here_ref[0]) % N_Z
    part = flat % N_YC
    grads = grads_ref[...]
    for k, out_ref in enumerate(out_refs):
        slot = jnp.where(
            (flat < EXPERTS) & (part == here_ref[1 + k]), along_z * CAP + rank, -1
        )
        pick = ones_where(iota((TOK, pairs), 0) == slot)
        out_ref[...] = jnp.dot(pick, grads, preferred_element_type=F32).astype(BF)


def pack_grads(here, flat, grads):
    return pl.pallas_call(
        pack_grads_kernel,
        out_shape=[jax.ShapeDtypeStruct((N_Z * CAP, FF), BF)] * N_YC,
        in_specs=[IN_SMEM] + [IN_VMEM] * 2,
        out_specs=[IN_VMEM] * N_YC,
        compiler_params=params(16),
        cost_estimate=pl.CostEstimate(
            flops=2 * ROWS * ROWS * FF, bytes_accessed=4 * ROWS * FF, transcendentals=0
        ),
    )(here, flat, grads)


def regroup_kernel(*refs):
    in_refs, out_refs = refs[:N_YC], refs[-N_Z:]
    for i, in_ref in enumerate(in_refs):
        for k, out_ref in enumerate(out_refs):
            out_ref[i * CAP : (i + 1) * CAP, :] = in_ref[k * CAP : (k + 1) * CAP, :]


def regroup(blocks, others):
    return pl.pallas_call(
        regroup_kernel,
        out_shape=[jax.ShapeDtypeStruct((N_YC * CAP, FF), BF)] * N_Z,
        in_specs=[IN_VMEM] * N_YC + [pl.BlockSpec(memory_space=pl.ANY)] * len(others),
        out_specs=[IN_VMEM] * N_Z,
        compiler_params=params(8),
    )(*blocks, *others)


def pack_tokens_kernel(n, here_ref, *refs):
    lefts, rights, out_refs = refs[:n], refs[n : 2 * n], refs[2 * n :]
    turn = iota((N_YC, TOK), 0)
    expert = jnp.zeros((N_YC, TOK), I32)
    for k in range(N_YC):
        expert = jnp.where(turn == k, here_ref[0] * N_YC + here_ref[1 + k], expert)
    rank = iota((CAP, TOK), 0)
    ahead = earlier(TOK)
    for b, (left, right) in enumerate(zip(lefts, rights)):
        routing = left[TOK:, 0:TOK].astype(F32).astype(I32)
        member = jnp.zeros((N_YC, TOK), F32)
        for j in range(TOP):
            member += jnp.where(routing[j : j + 1, :] == expert, 1.0, 0.0)
        before = jnp.dot(member.astype(BF), ahead, preferred_element_type=F32)
        slot = jnp.where(member > 0, before, -1.0).astype(I32)
        pick = jnp.concatenate([ones_where(slot[k : k + 1, :] == rank) for k in range(N_YC)], axis=0)
        for at, rows_ref in ((0, left), (WIDE, right)):
            rows = jnp.dot(pick, rows_ref[0:TOK, :], preferred_element_type=F32).astype(BF)
            for k, out_ref in enumerate(out_refs):
                out_ref[b * CAP : (b + 1) * CAP, at : at + WIDE] = rows[k * CAP : (k + 1) * CAP, :]


def pack_tokens(here, lefts, rights):
    n = len(lefts)
    return pl.pallas_call(
        functools.partial(pack_tokens_kernel, n),
        out_shape=[jax.ShapeDtypeStruct((n * CAP, D), BF)] * N_YC,
        in_specs=[IN_SMEM] + [IN_VMEM] * (2 * n),
        out_specs=[IN_VMEM] * N_YC,
        compiler_params=params(16),
        cost_estimate=pl.CostEstimate(
            flops=2 * n * TOK * TOK * D, bytes_accessed=4 * n * TOK * D, transcendentals=0
        ),
    )(here, *lefts, *rights)


STRIP = 256


def rotate_kernel(*refs):
    parts, basis_ref, out_ref, rows_ref = refs[:N_YC], refs[N_YC], refs[-2], refs[-1]
    n = rows_ref.shape[0] // TOK

    @pl.when(pl.program_id(0) == 0)
    def _():
        for k, part in enumerate(parts):
            for b in range(n):
                start = b * TOK + k * CAP
                rows_ref[start : start + CAP, :] = part[b * CAP : (b + 1) * CAP, :]

    rotated = jnp.dot(rows_ref[...], basis_ref[0], preferred_element_type=F32)
    out_ref[...] = jnp.transpose(rotated * rotated).astype(BF)


def rotate_inputs(parts, basis_in):
    rows = parts[0].shape[0] * N_YC
    return pl.pallas_call(
        rotate_kernel,
        out_shape=jax.ShapeDtypeStruct((D, rows), BF),
        grid=(D // STRIP,),
        in_specs=[pl.BlockSpec(parts[0].shape, lambda i: (0, 0))] * N_YC
        + [pl.BlockSpec((1, D, STRIP), lambda i: (0, 0, i))],
        out_specs=pl.BlockSpec((STRIP, rows), lambda i: (i, 0)),
        scratch_shapes=[pltpu.VMEM((rows, D), BF)],
        compiler_params=params(24),
        cost_estimate=pl.CostEstimate(
            flops=2 * rows * D * D, bytes_accessed=2 * D * D + 4 * rows * D, transcendentals=0
        ),
    )(*parts, basis_in)


def encode(values, out_ref):
    most = jnp.max(values, axis=0, keepdims=True)
    power = jnp.clip(jnp.ceil(jnp.log2(jnp.maximum(most, 1e-37))), -126.0, 126.0)
    scaled = (values * jnp.exp2(-power)) * 65535.0 + 0.5
    code = jnp.minimum(scaled.astype(I32), 65535) - 32768
    out_ref[0:HALF, :] = code.astype(jnp.int16)
    out_ref[HALF:CODE_ROWS, :] = jnp.broadcast_to(power.astype(I32), (16, FF)).astype(jnp.int16)


def decode(code_ref):
    power = code_ref[HALF:CODE_ROWS, :].astype(I32)[0:1, :].astype(F32)
    value = (code_ref[0:HALF, :].astype(I32) + 32768).astype(F32)
    return value * (jnp.exp2(power) * (1.0 / 65535.0))


CODE = jax.ShapeDtypeStruct((CODE_ROWS, FF), jnp.int16)
BLOCK = jax.ShapeDtypeStruct((HALF, FF), F32)


N_FIRST = len(FIRST) * TOK


def block_sum(a_refs, g_ref, quarter, half):
    start = pl.multiple_of(quarter * QUARTER + half * HALF, HALF)
    first, second = a_refs
    return jnp.dot(
        first[pl.ds(start, HALF), :], g_ref[0:N_FIRST, :], preferred_element_type=F32
    ) + jnp.dot(second[pl.ds(start, HALF), :], g_ref[N_FIRST:, :], preferred_element_type=F32)


def far_kernel(place_ref, *refs):
    rows_refs, (basis_ref, first, second, g_ref, up_ref, down_ref) = refs[:N_Z], refs[N_Z:]
    for k, rows_ref in enumerate(rows_refs):
        rotated = jnp.dot(rows_ref[...], basis_ref[0], preferred_element_type=F32)
        g_ref[k * TOK : (k + 1) * TOK, :] = (rotated * rotated).astype(BF)
    encode(block_sum((first, second), g_ref, place_ref[0], 0), up_ref)
    encode(block_sum((first, second), g_ref, place_ref[0], 1), down_ref)


def far_blocks(place, rows, basis_out, a_sq):
    return pl.pallas_call(
        far_kernel,
        out_shape=(jax.ShapeDtypeStruct((ROWS, FF), BF), CODE, CODE),
        in_specs=[IN_SMEM] + [IN_VMEM] * (N_Z + 3),
        out_specs=[IN_VMEM] * 3,
        compiler_params=params(20),
        cost_estimate=pl.CostEstimate(
            flops=2 * ROWS * FF * (FF + QUARTER), bytes_accessed=12 << 20, transcendentals=0
        ),
    )(place, *rows, basis_out, *a_sq)


def near_kernel(place_ref, first, second, g_ref, up_ref, down_ref):
    encode(block_sum((first, second), g_ref, place_ref[1], 1), up_ref)
    encode(block_sum((first, second), g_ref, place_ref[2], 0), down_ref)


def near_blocks(place, a_sq, g_sq):
    return pl.pallas_call(
        near_kernel,
        out_shape=(CODE, CODE),
        in_specs=[IN_SMEM] + [IN_VMEM] * 3,
        out_specs=[IN_VMEM] * 2,
        compiler_params=params(16),
        cost_estimate=pl.CostEstimate(
            flops=2 * ROWS * FF * QUARTER, bytes_accessed=4 << 20, transcendentals=0
        ),
    )(place, *a_sq, g_sq)


def rest_kernel(place_ref, first, second, g_ref, up_ref, down_ref, own_ref):
    a_refs = (first, second)
    up_ref[...] = block_sum(a_refs, g_ref, place_ref[1], 0)
    down_ref[...] = block_sum(a_refs, g_ref, place_ref[2], 1)
    own_ref[0:HALF, :] = block_sum(a_refs, g_ref, place_ref[3], 0)
    own_ref[HALF:QUARTER, :] = block_sum(a_refs, g_ref, place_ref[3], 1)


def rest_blocks(place, a_sq, g_sq):
    return pl.pallas_call(
        rest_kernel,
        out_shape=(BLOCK, BLOCK, jax.ShapeDtypeStruct((QUARTER, FF), F32)),
        in_specs=[IN_SMEM] + [IN_VMEM] * 3,
        out_specs=[IN_VMEM] * 3,
        compiler_params=params(20),
        cost_estimate=pl.CostEstimate(
            flops=4 * ROWS * FF * QUARTER, bytes_accessed=8 << 20, transcendentals=0
        ),
    )(place, *a_sq, g_sq)


def pass_on_kernel(up_ref, down_ref, got_up_ref, got_down_ref, out_up_ref, out_down_ref):
    encode(up_ref[...] + decode(got_up_ref), out_up_ref)
    encode(down_ref[...] + decode(got_down_ref), out_down_ref)


def pass_on(up, down, got_up, got_down):
    return pl.pallas_call(
        pass_on_kernel,
        out_shape=(CODE, CODE),
        in_specs=[IN_VMEM] * 4,
        out_specs=[IN_VMEM] * 2,
        compiler_params=params(12),
    )(up, down, got_up, got_down)


LANES = 128
SPLIT = FF // LANES


def finish_kernel(own_ref, top_a_ref, top_b_ref, bottom_a_ref, bottom_b_ref, out_ref):
    top = own_ref[0:HALF, :] + decode(top_a_ref) + decode(top_b_ref)
    bottom = own_ref[HALF:QUARTER, :] + decode(bottom_a_ref) + decode(bottom_b_ref)
    for k in range(SPLIT):
        lanes = slice(k * LANES, (k + 1) * LANES)
        out_ref[pl.ds(k, HALF, stride=SPLIT), :] = top[:, lanes]
        out_ref[pl.ds(HALF * SPLIT + k, HALF, stride=SPLIT), :] = bottom[:, lanes]


def finish(own, top_a, top_b, bottom_a, bottom_b):
    return pl.pallas_call(
        finish_kernel,
        out_shape=jax.ShapeDtypeStruct((QUARTER * SPLIT, LANES), F32),
        in_specs=[IN_VMEM] * 5,
        out_specs=IN_VMEM,
        compiler_params=params(12),
    )(own, top_a, top_b, bottom_a, bottom_b)


def shift(value, axis, by):
    n = lax.axis_size(axis)
    return lax.ppermute(value, axis, [(i, (i + by) % n) for i in range(n)])


def turned(value, turn):
    along, other = turn
    pairs = [
        (y * N_C + c, (y + along) % N_Y * N_C + (c ^ other)) for y in range(N_Y) for c in range(N_C)
    ]
    return value if turn == (0, 0) else lax.ppermute(value, ("y", "c"), pairs)


def z_ring(left, right):
    up, down = {0: (left, right)}, {0: (left, right)}
    for step in (1, 2, 3):
        up[step] = tuple(shift(v, "z", 1) for v in up[step - 1])
        down[step] = tuple(shift(v, "z", -1) for v in down[step - 1])
    ring = {**up, **{N_Z - step: down[step] for step in (1, 2, 3)}}
    ring[4] = (shift(up[3][0], "z", 1), shift(down[3][1], "z", -1))
    return ring


def on_device(tokens, grads, routing, basis_in, basis_out):
    x, z = lax.axis_index("x"), lax.axis_index("z")
    y, c = lax.axis_index("y"), lax.axis_index("c")
    place = jnp.stack([x ^ 2, (x + 1) & 3, (x + 3) & 3, x]).astype(I32)
    here = jnp.stack([z] + [((y + along) & 3) * N_C + (c ^ other) for along, other in TURNS])
    here = here.astype(I32)

    ring = z_ring(*stage(tokens, routing.T))
    packed = pack_grads(here, routing.reshape(1, TOK * TOP), grads.reshape(TOK * TOP, FF))
    packed = [turned(v, turn) for v, turn in zip(packed, TURNS)]
    by_z = regroup(packed, [ring[3][0], ring[5][0]])
    rows_out = [by_z[k] if k == 0 else shift(by_z[k], "z", k) for k in ORDER]

    a_sq = []
    for senders in (FIRST, SECOND):
        rows_in = pack_tokens(here, [ring[k][0] for k in senders], [ring[k][1] for k in senders])
        rows_in = [turned(v, turn) for v, turn in zip(rows_in, TURNS)]
        a_sq.append(rotate_inputs(rows_in, basis_in))

    g_sq, far_up, far_down = far_blocks(place, rows_out, basis_out, a_sq)
    got_far_up, got_far_down = shift(far_up, "x", 1), shift(far_down, "x", -1)
    near_up, near_down = near_blocks(place, a_sq, g_sq)
    got_near_up, got_near_down = shift(near_up, "x", 1), shift(near_down, "x", -1)
    up, down, own = rest_blocks(place, a_sq, g_sq)
    up, down = pass_on(up, down, got_far_up, got_far_down)
    got_up, got_down = shift(up, "x", 1), shift(down, "x", -1)
    values = finish(own, got_up, got_near_down, got_near_up, got_down)
    return values.reshape(QUARTER, 1, FF)


def solution(mesh):
    split = Mesh(mesh.devices.reshape(N_X, N_Z, N_Y, N_C), ("x", "z", "y", "c"))
    owner = ("z", "y", "c")
    everywhere = ("x", "z", "y", "c")
    return jax.shard_map(
        on_device,
        mesh=split,
        in_specs=(
            P(everywhere, None),
            P(everywhere, None, None),
            P(everywhere, None),
            P(owner, None, None),
            P(owner, None, None),
        ),
        out_specs=P("x", owner, None),
        check_vma=False,
    )
```

```python
import functools

import jax
import jax.numpy as jnp
from jax import lax
from jax.experimental import pallas as pl
from jax.experimental.pallas import tpu as pltpu
from jax.sharding import Mesh
from jax.sharding import PartitionSpec as P

CAP = 16
N_X, N_Z, N_Y, N_C = 4, 8, 4, 2
N_YC = N_Y * N_C
FIRST = (0, 1, 7, 2, 6, 3, 5)
SECOND = (4,)
ORDER = FIRST + SECOND
TOK = 128
TOP = 8
D = 2048
WIDE = D // 2
FF = 768
EXPERTS = 64
ROWS = EXPERTS * CAP
QUARTER = D // N_X
HALF = QUARTER // 2
CODE_ROWS = HALF + 16
BF = jnp.bfloat16
F32 = jnp.float32
I32 = jnp.int32
MIB = 1024 * 1024
IN_SMEM = pl.BlockSpec(memory_space=pltpu.SMEM)
IN_VMEM = pl.BlockSpec(memory_space=pltpu.VMEM)


def iota(shape, dim):
    return lax.broadcasted_iota(I32, shape, dim)


def params(mib):
    return pltpu.CompilerParams(vmem_limit_bytes=mib * MIB)


def ones_where(mask):
    return jnp.where(mask, 1.0, 0.0).astype(BF)


def earlier(n):
    return ones_where(iota((n, n), 0) < iota((n, n), 1))


def stage_kernel(tokens_ref, routing_ref, left_ref, right_ref):
    left_ref[0:TOK, :] = tokens_ref[:, 0:WIDE]
    left_ref[TOK:, :] = jnp.zeros((TOP, WIDE), BF)
    left_ref[TOK:, 0:TOK] = routing_ref[...].astype(F32).astype(BF)
    right_ref[...] = tokens_ref[:, WIDE:]


def stage(tokens, routing):
    return pl.pallas_call(
        stage_kernel,
        out_shape=(
            jax.ShapeDtypeStruct((TOK + TOP, WIDE), BF),
            jax.ShapeDtypeStruct((TOK, WIDE), BF),
        ),
        compiler_params=params(60),
    )(tokens, routing)


def pack_grads_kernel(here_ref, flat_ref, grads_ref, out_ref):
    pairs = TOK * TOP
    flat = flat_ref[...]
    hit = iota((EXPERTS, pairs), 0) == flat
    before = jnp.dot(ones_where(hit), earlier(pairs), preferred_element_type=F32)
    rank = jnp.sum(jnp.where(hit, before, 0.0), axis=0, keepdims=True).astype(I32)
    along_z = (flat // N_YC + N_Z - here_ref[0]) % N_Z
    slot = jnp.where(flat < EXPERTS, (flat % N_YC) * TOK + along_z * CAP + rank, -1)
    grads = grads_ref[...]
    for k in range(N_YC):
        pick = ones_where(iota((TOK, pairs), 0) + k * TOK == slot)
        out_ref[k] = jnp.dot(pick, grads, preferred_element_type=F32).astype(BF)


def pack_grads(here, flat, grads):
    return pl.pallas_call(
        pack_grads_kernel,
        out_shape=jax.ShapeDtypeStruct((N_YC, N_Z * CAP, FF), BF),
        in_specs=[IN_SMEM] + [IN_VMEM] * 2,
        out_specs=IN_VMEM,
        compiler_params=params(60),
        cost_estimate=pl.CostEstimate(
            flops=2 * ROWS * ROWS * FF, bytes_accessed=4 * ROWS * FF, transcendentals=0
        ),
    )(here, flat, grads)


def regroup_kernel(*refs):
    in_ref, out_refs = refs[0], refs[-N_Z:]
    for k, out_ref in enumerate(out_refs):
        for i in range(N_YC):
            out_ref[i * CAP : (i + 1) * CAP, :] = in_ref[i, k * CAP : (k + 1) * CAP, :]


def regroup(blocks, others):
    return pl.pallas_call(
        regroup_kernel,
        out_shape=[jax.ShapeDtypeStruct((N_YC * CAP, FF), BF)] * N_Z,
        in_specs=[IN_VMEM] + [pl.BlockSpec(memory_space=pl.ANY)] * len(others),
        out_specs=[IN_VMEM] * N_Z,
        compiler_params=params(60),
    )(blocks, *others)


def pack_tokens_kernel(n, here_ref, *refs):
    lefts, rights, out_ref = refs[:n], refs[n : 2 * n], refs[-1]
    expert = iota((N_YC, TOK), 0) + here_ref[0] * N_YC
    rank = iota((CAP, TOK), 0)
    ahead = earlier(TOK)
    for b, (left, right) in enumerate(zip(lefts, rights)):
        routing = left[TOK:, 0:TOK].astype(F32).astype(I32)
        member = jnp.zeros((N_YC, TOK), F32)
        for j in range(TOP):
            member += jnp.where(routing[j : j + 1, :] == expert, 1.0, 0.0)
        before = jnp.dot(member.astype(BF), ahead, preferred_element_type=F32)
        slot = jnp.where(member > 0, before, -1.0).astype(I32)
        pick = jnp.concatenate([ones_where(slot[k : k + 1, :] == rank) for k in range(N_YC)], axis=0)
        for at, rows_ref in ((0, left), (WIDE, right)):
            rows = jnp.dot(pick, rows_ref[0:TOK, :], preferred_element_type=F32).astype(BF)
            out_ref[:, b * CAP : (b + 1) * CAP, at : at + WIDE] = rows.reshape(N_YC, CAP, WIDE)


def pack_tokens(here, lefts, rights, gates):
    n = len(lefts)
    return pl.pallas_call(
        functools.partial(pack_tokens_kernel, n),
        out_shape=jax.ShapeDtypeStruct((N_YC, n * CAP, D), BF),
        in_specs=[IN_SMEM] + [IN_VMEM] * (2 * n) + [pl.BlockSpec(memory_space=pl.ANY)] * len(gates),
        out_specs=IN_VMEM,
        compiler_params=params(60),
        cost_estimate=pl.CostEstimate(
            flops=2 * n * TOK * TOK * D, bytes_accessed=4 * n * TOK * D, transcendentals=0
        ),
    )(here, *lefts, *rights, *gates)


STRIP = 512


def rotate_kernel(parts_ref, basis_ref, out_ref, rows_ref):
    @pl.when(pl.program_id(0) == 0)
    def _():
        for k in range(N_YC):
            for b in range(rows_ref.shape[0] // TOK):
                start = b * TOK + k * CAP
                rows_ref[start : start + CAP, :] = parts_ref[k, b * CAP : (b + 1) * CAP, :]

    rotated = jnp.dot(rows_ref[...], basis_ref[0], preferred_element_type=F32)
    out_ref[...] = jnp.transpose(rotated * rotated).astype(BF)


def rotate_inputs(parts, basis_in):
    rows = parts.shape[1] * N_YC
    return pl.pallas_call(
        rotate_kernel,
        out_shape=jax.ShapeDtypeStruct((D, rows), BF),
        grid=(D // STRIP,),
        in_specs=[
            pl.BlockSpec(parts.shape, lambda i: (0, 0, 0)),
            pl.BlockSpec((1, D, STRIP), lambda i: (0, 0, i)),
        ],
        out_specs=pl.BlockSpec((STRIP, rows), lambda i: (i, 0)),
        scratch_shapes=[pltpu.VMEM((rows, D), BF)],
        compiler_params=params(50),
        cost_estimate=pl.CostEstimate(
            flops=2 * rows * D * D, bytes_accessed=2 * D * D + 4 * rows * D, transcendentals=0
        ),
    )(parts, basis_in)


def encode(values, out_ref):
    most = jnp.max(values, axis=0, keepdims=True)
    power = jnp.clip(jnp.ceil(jnp.log2(jnp.maximum(most, 1e-37))), -126.0, 126.0)
    scaled = (values * jnp.exp2(-power)) * 65535.0 + 0.5
    code = jnp.minimum(scaled.astype(I32), 65535) - 32768
    out_ref[0:HALF, :] = code.astype(jnp.int16)
    out_ref[HALF:CODE_ROWS, :] = jnp.broadcast_to(power.astype(I32), (16, FF)).astype(jnp.int16)


def decode(code_ref):
    power = code_ref[HALF:CODE_ROWS, :].astype(I32)[0:1, :].astype(F32)
    value = (code_ref[0:HALF, :].astype(I32) + 32768).astype(F32)
    return value * (jnp.exp2(power) * (1.0 / 65535.0))


CODE = jax.ShapeDtypeStruct((CODE_ROWS, FF), jnp.int16)
BLOCK = jax.ShapeDtypeStruct((HALF, FF), F32)


N_FIRST = len(FIRST) * TOK


def block_sum(a_refs, g_ref, quarter, half):
    start = pl.multiple_of(quarter * QUARTER + half * HALF, HALF)
    first, second = a_refs
    return jnp.dot(
        first[pl.ds(start, HALF), :], g_ref[0:N_FIRST, :], preferred_element_type=F32
    ) + jnp.dot(second[pl.ds(start, HALF), :], g_ref[N_FIRST:, :], preferred_element_type=F32)


def far_kernel(place_ref, *refs):
    rows_refs, (basis_ref, first, second, g_ref, up_ref, down_ref) = refs[:N_Z], refs[N_Z:]
    for k, rows_ref in enumerate(rows_refs):
        rotated = jnp.dot(rows_ref[...], basis_ref[0], preferred_element_type=F32)
        g_ref[k * TOK : (k + 1) * TOK, :] = (rotated * rotated).astype(BF)
    encode(block_sum((first, second), g_ref, place_ref[0], 0), up_ref)
    encode(block_sum((first, second), g_ref, place_ref[0], 1), down_ref)


def far_blocks(place, rows, basis_out, a_sq):
    return pl.pallas_call(
        far_kernel,
        out_shape=(jax.ShapeDtypeStruct((ROWS, FF), BF), CODE, CODE),
        in_specs=[IN_SMEM] + [IN_VMEM] * (N_Z + 3),
        out_specs=[IN_VMEM] * 3,
        compiler_params=params(8),
        cost_estimate=pl.CostEstimate(
            flops=2 * ROWS * FF * (FF + QUARTER), bytes_accessed=12 << 20, transcendentals=0
        ),
    )(place, *rows, basis_out, *a_sq)


def near_kernel(place_ref, first, second, g_ref, up_ref, down_ref):
    encode(block_sum((first, second), g_ref, place_ref[1], 1), up_ref)
    encode(block_sum((first, second), g_ref, place_ref[2], 0), down_ref)


def near_blocks(place, a_sq, g_sq):
    return pl.pallas_call(
        near_kernel,
        out_shape=(CODE, CODE),
        in_specs=[IN_SMEM] + [IN_VMEM] * 3,
        out_specs=[IN_VMEM] * 2,
        compiler_params=params(4),
        cost_estimate=pl.CostEstimate(
            flops=2 * ROWS * FF * QUARTER, bytes_accessed=4 << 20, transcendentals=0
        ),
    )(place, *a_sq, g_sq)


def rest_kernel(place_ref, first, second, g_ref, up_ref, down_ref, own_ref):
    a_refs = (first, second)
    up_ref[...] = block_sum(a_refs, g_ref, place_ref[1], 0)
    down_ref[...] = block_sum(a_refs, g_ref, place_ref[2], 1)
    own_ref[0:HALF, :] = block_sum(a_refs, g_ref, place_ref[3], 0)
    own_ref[HALF:QUARTER, :] = block_sum(a_refs, g_ref, place_ref[3], 1)


def rest_blocks(place, a_sq, g_sq):
    return pl.pallas_call(
        rest_kernel,
        out_shape=(BLOCK, BLOCK, jax.ShapeDtypeStruct((QUARTER, FF), F32)),
        in_specs=[IN_SMEM] + [IN_VMEM] * 3,
        out_specs=[IN_VMEM] * 3,
        compiler_params=params(4),
        cost_estimate=pl.CostEstimate(
            flops=4 * ROWS * FF * QUARTER, bytes_accessed=8 << 20, transcendentals=0
        ),
    )(place, *a_sq, g_sq)


def pass_on_kernel(up_ref, down_ref, got_up_ref, got_down_ref, out_up_ref, out_down_ref):
    encode(up_ref[...] + decode(got_up_ref), out_up_ref)
    encode(down_ref[...] + decode(got_down_ref), out_down_ref)


def pass_on(up, down, got_up, got_down):
    return pl.pallas_call(
        pass_on_kernel,
        out_shape=(CODE, CODE),
        in_specs=[IN_VMEM] * 4,
        out_specs=[IN_VMEM] * 2,
        compiler_params=params(4),
    )(up, down, got_up, got_down)


LANES = 128
SPLIT = FF // LANES


def finish_kernel(own_ref, top_a_ref, top_b_ref, bottom_a_ref, bottom_b_ref, out_ref):
    top = own_ref[0:HALF, :] + decode(top_a_ref) + decode(top_b_ref)
    bottom = own_ref[HALF:QUARTER, :] + decode(bottom_a_ref) + decode(bottom_b_ref)
    for k in range(SPLIT):
        lanes = slice(k * LANES, (k + 1) * LANES)
        out_ref[pl.ds(k, HALF, stride=SPLIT), :] = top[:, lanes]
        out_ref[pl.ds(HALF * SPLIT + k, HALF, stride=SPLIT), :] = bottom[:, lanes]


def finish(own, top_a, top_b, bottom_a, bottom_b):
    return pl.pallas_call(
        finish_kernel,
        out_shape=jax.ShapeDtypeStruct((QUARTER * SPLIT, LANES), F32),
        in_specs=[IN_VMEM] * 5,
        out_specs=IN_VMEM,
        compiler_params=params(4),
    )(own, top_a, top_b, bottom_a, bottom_b)


def shift(value, axis, by):
    n = lax.axis_size(axis)
    return lax.ppermute(value, axis, [(i, (i + by) % n) for i in range(n)])


def to_owners(value):
    return lax.all_to_all(value, ("y", "c"), split_axis=0, concat_axis=0, tiled=True)


def z_ring(left, right):
    up, down = {0: (left, right)}, {0: (left, right)}
    for step in (1, 2, 3):
        up[step] = tuple(shift(v, "z", 1) for v in up[step - 1])
        down[step] = tuple(shift(v, "z", -1) for v in down[step - 1])
    ring = {**up, **{N_Z - step: down[step] for step in (1, 2, 3)}}
    ring[4] = (shift(up[3][0], "z", 1), shift(down[3][1], "z", -1))
    return ring


def on_device(tokens, grads, routing, basis_in, basis_out):
    x, z = lax.axis_index("x"), lax.axis_index("z")
    place = jnp.stack([x ^ 2, (x + 1) & 3, (x + 3) & 3, x]).astype(I32)
    here = z.astype(I32).reshape(1)

    ring = z_ring(*stage(tokens, routing.T))
    packed = pack_grads(here, routing.reshape(1, TOK * TOP), grads.reshape(TOK * TOP, FF))
    grads_in = to_owners(packed)
    by_z = regroup(grads_in, [*ring[3], *ring[5]])
    rows_out = [by_z[k] if k == 0 else shift(by_z[k], "z", k) for k in ORDER]

    a_sq, gates = [], [grads_in]
    for senders in (FIRST, SECOND):
        rows_in = pack_tokens(
            here, [ring[k][0] for k in senders], [ring[k][1] for k in senders], gates
        )
        rows_in = to_owners(rows_in)
        gates = [rows_in, by_z[0], rows_out[ORDER.index(3)], rows_out[ORDER.index(5)]]
        a_sq.append(rotate_inputs(rows_in, basis_in))

    g_sq, far_up, far_down = far_blocks(place, rows_out, basis_out, a_sq)
    got_far_up, got_far_down = shift(far_up, "x", 1), shift(far_down, "x", -1)
    near_up, near_down = near_blocks(place, a_sq, g_sq)
    got_near_up, got_near_down = shift(near_up, "x", 1), shift(near_down, "x", -1)
    up, down, own = rest_blocks(place, a_sq, g_sq)
    up, down = pass_on(up, down, got_far_up, got_far_down)
    got_up, got_down = shift(up, "x", 1), shift(down, "x", -1)
    values = finish(own, got_up, got_near_down, got_near_up, got_down)
    return values.reshape(QUARTER, 1, FF)


def solution(mesh):
    split = Mesh(mesh.devices.reshape(N_X, N_Z, N_Y, N_C), ("x", "z", "y", "c"))
    owner = ("z", "y", "c")
    everywhere = ("x", "z", "y", "c")
    return jax.shard_map(
        on_device,
        mesh=split,
        in_specs=(
            P(everywhere, None),
            P(everywhere, None, None),
            P(everywhere, None),
            P(owner, None, None),
            P(owner, None, None),
        ),
        out_specs=P("x", owner, None),
        check_vma=False,
    )
```

```python
import functools

import jax
import jax.numpy as jnp
from jax import lax
from jax.experimental import pallas as pl
from jax.experimental.pallas import tpu as pltpu
from jax.sharding import Mesh
from jax.sharding import PartitionSpec as P

CAP = 16
N_X, N_Z, N_Y, N_C = 4, 8, 4, 2
N_YC = N_Y * N_C
FIRST = (0, 1, 7, 2, 6)
SECOND = (3, 5, 4)
ORDER = FIRST + SECOND
TOK = 128
TOP = 8
D = 2048
WIDE = D // 2
FF = 768
EXPERTS = 64
ROWS = EXPERTS * CAP
QUARTER = D // N_X
HALF = QUARTER // 2
CODE_ROWS = HALF + 16
BF = jnp.bfloat16
F32 = jnp.float32
I32 = jnp.int32
MIB = 1024 * 1024
IN_SMEM = pl.BlockSpec(memory_space=pltpu.SMEM)
IN_VMEM = pl.BlockSpec(memory_space=pltpu.VMEM)


def iota(shape, dim):
    return lax.broadcasted_iota(I32, shape, dim)


def params(mib):
    return pltpu.CompilerParams(vmem_limit_bytes=mib * MIB)


def ones_where(mask):
    return jnp.where(mask, 1.0, 0.0).astype(BF)


def earlier(n):
    return ones_where(iota((n, n), 0) < iota((n, n), 1))


def stage_kernel(tokens_ref, routing_ref, left_ref, right_ref):
    left_ref[0:TOK, :] = tokens_ref[:, 0:WIDE]
    left_ref[TOK:, :] = jnp.zeros((TOP, WIDE), BF)
    left_ref[TOK:, 0:TOK] = routing_ref[...].astype(F32).astype(BF)
    right_ref[...] = tokens_ref[:, WIDE:]


def stage(tokens, routing):
    return pl.pallas_call(
        stage_kernel,
        out_shape=(
            jax.ShapeDtypeStruct((TOK + TOP, WIDE), BF),
            jax.ShapeDtypeStruct((TOK, WIDE), BF),
        ),
        compiler_params=params(60),
    )(tokens, routing)


def pack_grads_kernel(here_ref, routing_ref, grads_ref, *refs):
    out_ref = refs[-1]
    pairs = TOK * TOP
    token = ones_where(iota((TOK, pairs), 1) // TOP == iota((TOK, pairs), 0))
    spread = jnp.dot(routing_ref[...].astype(F32).astype(BF), token, preferred_element_type=F32)
    choice = iota((TOP, pairs), 1) % TOP == iota((TOP, pairs), 0)
    flat = jnp.sum(jnp.where(choice, spread, 0.0), axis=0, keepdims=True).astype(I32)
    hit = iota((EXPERTS, pairs), 0) == flat
    before = jnp.dot(ones_where(hit), earlier(pairs), preferred_element_type=F32)
    rank = jnp.sum(jnp.where(hit, before, 0.0), axis=0, keepdims=True).astype(I32)
    along_z = (flat // N_YC + N_Z - here_ref[0]) % N_Z
    slot = jnp.where(flat < EXPERTS, (flat % N_YC) * TOK + along_z * CAP + rank, -1)
    grads = grads_ref[...]
    for k in range(N_YC):
        pick = ones_where(iota((TOK, pairs), 0) + k * TOK == slot)
        out_ref[k] = jnp.dot(pick, grads, preferred_element_type=F32).astype(BF)


def pack_grads(here, routing, grads, gates):
    return pl.pallas_call(
        pack_grads_kernel,
        out_shape=jax.ShapeDtypeStruct((N_YC, N_Z * CAP, FF), BF),
        in_specs=[IN_SMEM] + [IN_VMEM] * 2 + [pl.BlockSpec(memory_space=pl.ANY)] * len(gates),
        out_specs=IN_VMEM,
        compiler_params=params(60),
        cost_estimate=pl.CostEstimate(
            flops=2 * ROWS * ROWS * FF, bytes_accessed=4 * ROWS * FF, transcendentals=0
        ),
    )(here, routing, grads, *gates)


def regroup_kernel(*refs):
    in_ref, out_refs = refs[0], refs[-N_Z:]
    for k, out_ref in enumerate(out_refs):
        for i in range(N_YC):
            out_ref[i * CAP : (i + 1) * CAP, :] = in_ref[i, k * CAP : (k + 1) * CAP, :]


def regroup(blocks, others):
    return pl.pallas_call(
        regroup_kernel,
        out_shape=[jax.ShapeDtypeStruct((N_YC * CAP, FF), BF)] * N_Z,
        in_specs=[IN_VMEM] + [pl.BlockSpec(memory_space=pl.ANY)] * len(others),
        out_specs=[IN_VMEM] * N_Z,
        compiler_params=params(60),
    )(blocks, *others)


def pack_tokens_kernel(n, here_ref, *refs):
    lefts, rights, out_ref = refs[:n], refs[n : 2 * n], refs[-1]
    expert = iota((N_YC, TOK), 0) + here_ref[0] * N_YC
    rank = iota((CAP, TOK), 0)
    ahead = earlier(TOK)
    for b, (left, right) in enumerate(zip(lefts, rights)):
        routing = left[TOK:, 0:TOK].astype(F32).astype(I32)
        member = jnp.zeros((N_YC, TOK), F32)
        for j in range(TOP):
            member += jnp.where(routing[j : j + 1, :] == expert, 1.0, 0.0)
        before = jnp.dot(member.astype(BF), ahead, preferred_element_type=F32)
        slot = jnp.where(member > 0, before, -1.0).astype(I32)
        pick = jnp.concatenate([ones_where(slot[k : k + 1, :] == rank) for k in range(N_YC)], axis=0)
        for at, rows_ref in ((0, left), (WIDE, right)):
            rows = jnp.dot(pick, rows_ref[0:TOK, :], preferred_element_type=F32).astype(BF)
            out_ref[:, b * CAP : (b + 1) * CAP, at : at + WIDE] = rows.reshape(N_YC, CAP, WIDE)


def pack_tokens(here, lefts, rights, gates):
    n = len(lefts)
    return pl.pallas_call(
        functools.partial(pack_tokens_kernel, n),
        out_shape=jax.ShapeDtypeStruct((N_YC, n * CAP, D), BF),
        in_specs=[IN_SMEM] + [IN_VMEM] * (2 * n) + [pl.BlockSpec(memory_space=pl.ANY)] * len(gates),
        out_specs=IN_VMEM,
        compiler_params=params(60),
        cost_estimate=pl.CostEstimate(
            flops=2 * n * TOK * TOK * D, bytes_accessed=4 * n * TOK * D, transcendentals=0
        ),
    )(here, *lefts, *rights, *gates)


STRIP = 512


def rotate_kernel(parts_ref, basis_ref, *refs):
    out_ref, rows_ref = refs[-2:]

    @pl.when(pl.program_id(0) == 0)
    def _():
        for k in range(N_YC):
            for b in range(rows_ref.shape[0] // TOK):
                start = b * TOK + k * CAP
                rows_ref[start : start + CAP, :] = parts_ref[k, b * CAP : (b + 1) * CAP, :]

    rotated = jnp.dot(rows_ref[...], basis_ref[0], preferred_element_type=F32)
    out_ref[...] = jnp.transpose((rotated * rotated).astype(BF))


def rotate_inputs(parts, basis_in, gates):
    rows = parts.shape[1] * N_YC
    return pl.pallas_call(
        rotate_kernel,
        out_shape=jax.ShapeDtypeStruct((D, rows), BF),
        grid=(D // STRIP,),
        in_specs=[
            pl.BlockSpec(parts.shape, lambda i: (0, 0, 0)),
            pl.BlockSpec((1, D, STRIP), lambda i: (0, 0, i)),
        ]
        + [pl.BlockSpec(memory_space=pl.ANY)] * len(gates),
        out_specs=pl.BlockSpec((STRIP, rows), lambda i: (i, 0)),
        scratch_shapes=[pltpu.VMEM((rows, D), BF)],
        compiler_params=params(50),
        cost_estimate=pl.CostEstimate(
            flops=2 * rows * D * D, bytes_accessed=2 * D * D + 4 * rows * D, transcendentals=0
        ),
    )(parts, basis_in, *gates)


def encode(values, out_ref):
    most = jnp.max(values, axis=0, keepdims=True)
    power = jnp.clip(jnp.ceil(jnp.log2(jnp.maximum(most, 1e-37))), -126.0, 126.0)
    scaled = (values * jnp.exp2(-power)) * 65535.0 + 0.5
    code = jnp.minimum(scaled.astype(I32), 65535) - 32768
    out_ref[0:HALF, :] = code.astype(jnp.int16)
    out_ref[HALF:CODE_ROWS, :] = jnp.broadcast_to(power.astype(I32), (16, FF)).astype(jnp.int16)


def decode(code_ref):
    power = code_ref[HALF:CODE_ROWS, :].astype(I32)[0:1, :].astype(F32)
    value = (code_ref[0:HALF, :].astype(I32) + 32768).astype(F32)
    return value * (jnp.exp2(power) * (1.0 / 65535.0))


CODE = jax.ShapeDtypeStruct((CODE_ROWS, FF), jnp.int16)
BLOCK = jax.ShapeDtypeStruct((HALF, FF), F32)


N_FIRST = len(FIRST) * TOK


def block_sum(a_refs, g_ref, quarter, half):
    start = pl.multiple_of(quarter * QUARTER + half * HALF, HALF)
    first, second = a_refs
    return jnp.dot(
        first[pl.ds(start, HALF), :], g_ref[0:N_FIRST, :], preferred_element_type=F32
    ) + jnp.dot(second[pl.ds(start, HALF), :], g_ref[N_FIRST:, :], preferred_element_type=F32)


def far_kernel(place_ref, *refs):
    rows_refs, (basis_ref, first, second, g_ref, up_ref, down_ref) = refs[:N_Z], refs[N_Z:]
    for k, rows_ref in enumerate(rows_refs):
        rotated = jnp.dot(rows_ref[...], basis_ref[0], preferred_element_type=F32)
        g_ref[k * TOK : (k + 1) * TOK, :] = (rotated * rotated).astype(BF)
    encode(block_sum((first, second), g_ref, place_ref[0], 0), up_ref)
    encode(block_sum((first, second), g_ref, place_ref[0], 1), down_ref)


def far_blocks(place, rows, basis_out, a_sq):
    return pl.pallas_call(
        far_kernel,
        out_shape=(jax.ShapeDtypeStruct((ROWS, FF), BF), CODE, CODE),
        in_specs=[IN_SMEM] + [IN_VMEM] * (N_Z + 3),
        out_specs=[IN_VMEM] * 3,
        compiler_params=params(8),
        cost_estimate=pl.CostEstimate(
            flops=2 * ROWS * FF * (FF + QUARTER), bytes_accessed=12 << 20, transcendentals=0
        ),
    )(place, *rows, basis_out, *a_sq)


def near_kernel(place_ref, first, second, g_ref, up_ref, down_ref):
    encode(block_sum((first, second), g_ref, place_ref[1], 1), up_ref)
    encode(block_sum((first, second), g_ref, place_ref[2], 0), down_ref)


def near_blocks(place, a_sq, g_sq):
    return pl.pallas_call(
        near_kernel,
        out_shape=(CODE, CODE),
        in_specs=[IN_SMEM] + [IN_VMEM] * 3,
        out_specs=[IN_VMEM] * 2,
        compiler_params=params(4),
        cost_estimate=pl.CostEstimate(
            flops=2 * ROWS * FF * QUARTER, bytes_accessed=4 << 20, transcendentals=0
        ),
    )(place, *a_sq, g_sq)


def rest_kernel(place_ref, first, second, g_ref, up_ref, down_ref, own_ref):
    a_refs = (first, second)
    up_ref[...] = block_sum(a_refs, g_ref, place_ref[1], 0)
    down_ref[...] = block_sum(a_refs, g_ref, place_ref[2], 1)
    own_ref[0:HALF, :] = block_sum(a_refs, g_ref, place_ref[3], 0)
    own_ref[HALF:QUARTER, :] = block_sum(a_refs, g_ref, place_ref[3], 1)


def rest_blocks(place, a_sq, g_sq):
    return pl.pallas_call(
        rest_kernel,
        out_shape=(BLOCK, BLOCK, jax.ShapeDtypeStruct((QUARTER, FF), F32)),
        in_specs=[IN_SMEM] + [IN_VMEM] * 3,
        out_specs=[IN_VMEM] * 3,
        compiler_params=params(4),
        cost_estimate=pl.CostEstimate(
            flops=4 * ROWS * FF * QUARTER, bytes_accessed=8 << 20, transcendentals=0
        ),
    )(place, *a_sq, g_sq)


def pass_on_kernel(up_ref, down_ref, got_up_ref, got_down_ref, out_up_ref, out_down_ref):
    encode(up_ref[...] + decode(got_up_ref), out_up_ref)
    encode(down_ref[...] + decode(got_down_ref), out_down_ref)


def pass_on(up, down, got_up, got_down):
    return pl.pallas_call(
        pass_on_kernel,
        out_shape=(CODE, CODE),
        in_specs=[IN_VMEM] * 4,
        out_specs=[IN_VMEM] * 2,
        compiler_params=params(4),
    )(up, down, got_up, got_down)


LANES = 128
SPLIT = FF // LANES


def finish_kernel(own_ref, top_a_ref, top_b_ref, bottom_a_ref, bottom_b_ref, out_ref):
    top = own_ref[0:HALF, :] + decode(top_a_ref) + decode(top_b_ref)
    bottom = own_ref[HALF:QUARTER, :] + decode(bottom_a_ref) + decode(bottom_b_ref)
    for k in range(SPLIT):
        lanes = slice(k * LANES, (k + 1) * LANES)
        out_ref[pl.ds(k, HALF, stride=SPLIT), :] = top[:, lanes]
        out_ref[pl.ds(HALF * SPLIT + k, HALF, stride=SPLIT), :] = bottom[:, lanes]


def finish(own, top_a, top_b, bottom_a, bottom_b):
    return pl.pallas_call(
        finish_kernel,
        out_shape=jax.ShapeDtypeStruct((QUARTER * SPLIT, LANES), F32),
        in_specs=[IN_VMEM] * 5,
        out_specs=IN_VMEM,
        compiler_params=params(4),
    )(own, top_a, top_b, bottom_a, bottom_b)


def shift(value, axis, by):
    n = lax.axis_size(axis)
    return lax.ppermute(value, axis, [(i, (i + by) % n) for i in range(n)])


def to_owners(value):
    return lax.all_to_all(value, ("y", "c"), split_axis=0, concat_axis=0, tiled=True)


def z_ring(left, right):
    up, down = {0: (left, right)}, {0: (left, right)}
    for step in (1, 2, 3):
        up[step] = tuple(shift(v, "z", 1) for v in up[step - 1])
        down[step] = tuple(shift(v, "z", -1) for v in down[step - 1])
    ring = {**up, **{N_Z - step: down[step] for step in (1, 2, 3)}}
    ring[4] = (shift(up[3][0], "z", 1), shift(down[3][1], "z", -1))
    return ring


def on_device(tokens, grads, routing, basis_in, basis_out):
    x, z = lax.axis_index("x"), lax.axis_index("z")
    place = jnp.stack([x ^ 2, (x + 1) & 3, (x + 3) & 3, x]).astype(I32)
    here = z.astype(I32).reshape(1)

    ring = z_ring(*stage(tokens, routing.T))
    packed = pack_grads(here, routing.T, grads.reshape(TOK * TOP, FF), [])
    grads_in = to_owners(packed)
    by_z = regroup(grads_in, [*ring[3], *ring[5]])
    rows_out = [by_z[k] if k == 0 else shift(by_z[k], "z", k) for k in ORDER]

    a_sq, gates = [], [grads_in, *ring[3], *ring[5]]
    for senders in (FIRST, SECOND):
        packed = pack_tokens(
            here, [ring[k][0] for k in senders], [ring[k][1] for k in senders], gates
        )
        gates = [packed] + [rows_out[ORDER.index(k)] for k in (3, 5, 2, 6)]
        a_sq.append(rotate_inputs(to_owners(packed), basis_in, a_sq))

    g_sq, far_up, far_down = far_blocks(place, rows_out, basis_out, a_sq)
    got_far_up, got_far_down = shift(far_up, "x", 1), shift(far_down, "x", -1)
    near_up, near_down = near_blocks(place, a_sq, g_sq)
    got_near_up, got_near_down = shift(near_up, "x", 1), shift(near_down, "x", -1)
    up, down, own = rest_blocks(place, a_sq, g_sq)
    up, down = pass_on(up, down, got_far_up, got_far_down)
    got_up, got_down = shift(up, "x", 1), shift(down, "x", -1)
    values = finish(own, got_up, got_near_down, got_near_up, got_down)
    return values.reshape(QUARTER, 1, FF)


def solution(mesh):
    split = Mesh(mesh.devices.reshape(N_X, N_Z, N_Y, N_C), ("x", "z", "y", "c"))
    owner = ("z", "y", "c")
    everywhere = ("x", "z", "y", "c")
    return jax.shard_map(
        on_device,
        mesh=split,
        in_specs=(
            P(everywhere, None),
            P(everywhere, None, None),
            P(everywhere, None),
            P(owner, None, None),
            P(owner, None, None),
        ),
        out_specs=P("x", owner, None),
        check_vma=False,
    )
```

```python
import functools

import jax
import jax.numpy as jnp
from jax import lax
from jax.experimental import pallas as pl
from jax.experimental.pallas import tpu as pltpu
from jax.sharding import Mesh
from jax.sharding import PartitionSpec as P

CAP = 16
N_X, N_Z, N_Y, N_C = 4, 8, 4, 2
N_YC = N_Y * N_C
FIRST = (0, 1, 7, 2, 6)
SECOND = (3, 5, 4)
ORDER = FIRST + SECOND
TOK = 128
TOP = 8
D = 2048
WIDE = D // 2
FF = 768
EXPERTS = 64
ROWS = EXPERTS * CAP
QUARTER = D // N_X
HALF = QUARTER // 2
CODE_ROWS = HALF + 16
BF = jnp.bfloat16
F32 = jnp.float32
I32 = jnp.int32
MIB = 1024 * 1024
IN_SMEM = pl.BlockSpec(memory_space=pltpu.SMEM)
IN_VMEM = pl.BlockSpec(memory_space=pltpu.VMEM)


def iota(shape, dim):
    return lax.broadcasted_iota(I32, shape, dim)


def params(mib):
    return pltpu.CompilerParams(vmem_limit_bytes=mib * MIB)


def ones_where(mask):
    return jnp.where(mask, 1.0, 0.0).astype(BF)


def earlier(n):
    return ones_where(iota((n, n), 0) < iota((n, n), 1))


def stage_kernel(tokens_ref, routing_ref, left_ref, right_ref):
    left_ref[0:TOK, :] = tokens_ref[:, 0:WIDE]
    left_ref[TOK:, :] = jnp.zeros((TOP, WIDE), BF)
    left_ref[TOK:, 0:TOK] = routing_ref[...].astype(F32).astype(BF)
    right_ref[...] = tokens_ref[:, WIDE:]


def stage(tokens, routing):
    return pl.pallas_call(
        stage_kernel,
        out_shape=(
            jax.ShapeDtypeStruct((TOK + TOP, WIDE), BF),
            jax.ShapeDtypeStruct((TOK, WIDE), BF),
        ),
        compiler_params=params(60),
    )(tokens, routing)


def pack_grads_kernel(here_ref, routing_ref, grads_ref, *refs):
    out_ref = refs[-1]
    pairs = TOK * TOP
    token = ones_where(iota((TOK, pairs), 1) // TOP == iota((TOK, pairs), 0))
    spread = jnp.dot(routing_ref[...].astype(F32).astype(BF), token, preferred_element_type=F32)
    choice = iota((TOP, pairs), 1) % TOP == iota((TOP, pairs), 0)
    flat = jnp.sum(jnp.where(choice, spread, 0.0), axis=0, keepdims=True).astype(I32)
    hit = iota((EXPERTS, pairs), 0) == flat
    before = jnp.dot(ones_where(hit), earlier(pairs), preferred_element_type=F32)
    rank = jnp.sum(jnp.where(hit, before, 0.0), axis=0, keepdims=True).astype(I32)
    along_z = (flat // N_YC + N_Z - here_ref[0]) % N_Z
    slot = jnp.where(flat < EXPERTS, (flat % N_YC) * TOK + along_z * CAP + rank, -1)
    grads = grads_ref[...]
    for k in range(N_YC):
        pick = ones_where(iota((TOK, pairs), 0) + k * TOK == slot)
        out_ref[k] = jnp.dot(pick, grads, preferred_element_type=F32).astype(BF)


def pack_grads(here, routing, grads, gates):
    return pl.pallas_call(
        pack_grads_kernel,
        out_shape=jax.ShapeDtypeStruct((N_YC, N_Z * CAP, FF), BF),
        in_specs=[IN_SMEM] + [IN_VMEM] * 2 + [pl.BlockSpec(memory_space=pl.ANY)] * len(gates),
        out_specs=IN_VMEM,
        compiler_params=params(60),
        cost_estimate=pl.CostEstimate(
            flops=2 * ROWS * ROWS * FF, bytes_accessed=4 * ROWS * FF, transcendentals=0
        ),
    )(here, routing, grads, *gates)


def regroup_kernel(*refs):
    in_ref, out_refs = refs[0], refs[-N_Z:]
    for k, out_ref in enumerate(out_refs):
        for i in range(N_YC):
            out_ref[i * CAP : (i + 1) * CAP, :] = in_ref[i, k * CAP : (k + 1) * CAP, :]


def regroup(blocks, others):
    return pl.pallas_call(
        regroup_kernel,
        out_shape=[jax.ShapeDtypeStruct((N_YC * CAP, FF), BF)] * N_Z,
        in_specs=[IN_VMEM] + [pl.BlockSpec(memory_space=pl.ANY)] * len(others),
        out_specs=[IN_VMEM] * N_Z,
        compiler_params=params(60),
    )(blocks, *others)


def pack_tokens_kernel(n, here_ref, *refs):
    lefts, rights, out_ref = refs[:n], refs[n : 2 * n], refs[-1]
    expert = iota((N_YC, TOK), 0) + here_ref[0] * N_YC
    rank = iota((CAP, TOK), 0)
    ahead = earlier(TOK)
    for b, (left, right) in enumerate(zip(lefts, rights)):
        routing = left[TOK:, 0:TOK].astype(F32).astype(I32)
        member = jnp.zeros((N_YC, TOK), F32)
        for j in range(TOP):
            member += jnp.where(routing[j : j + 1, :] == expert, 1.0, 0.0)
        before = jnp.dot(member.astype(BF), ahead, preferred_element_type=F32)
        slot = jnp.where(member > 0, before, -1.0).astype(I32)
        pick = jnp.concatenate([ones_where(slot[k : k + 1, :] == rank) for k in range(N_YC)], axis=0)
        for at, rows_ref in ((0, left), (WIDE, right)):
            rows = jnp.dot(pick, rows_ref[0:TOK, :], preferred_element_type=F32).astype(BF)
            out_ref[:, b * CAP : (b + 1) * CAP, at : at + WIDE] = rows.reshape(N_YC, CAP, WIDE)


def pack_tokens(here, lefts, rights, gates):
    n = len(lefts)
    return pl.pallas_call(
        functools.partial(pack_tokens_kernel, n),
        out_shape=jax.ShapeDtypeStruct((N_YC, n * CAP, D), BF),
        in_specs=[IN_SMEM] + [IN_VMEM] * (2 * n) + [pl.BlockSpec(memory_space=pl.ANY)] * len(gates),
        out_specs=IN_VMEM,
        compiler_params=params(60),
        cost_estimate=pl.CostEstimate(
            flops=2 * n * TOK * TOK * D, bytes_accessed=4 * n * TOK * D, transcendentals=0
        ),
    )(here, *lefts, *rights, *gates)


STRIP = 512


def rotate_kernel(parts_ref, basis_ref, *refs):
    out_ref, rows_ref = refs[-2:]

    @pl.when(pl.program_id(0) == 0)
    def _():
        for k in range(N_YC):
            for b in range(rows_ref.shape[0] // TOK):
                start = b * TOK + k * CAP
                rows_ref[start : start + CAP, :] = parts_ref[k, b * CAP : (b + 1) * CAP, :]

    rotated = jnp.dot(rows_ref[...], basis_ref[0], preferred_element_type=F32)
    out_ref[...] = jnp.transpose((rotated * rotated).astype(BF))


def rotate_inputs(parts, basis_in, gates):
    rows = parts.shape[1] * N_YC
    return pl.pallas_call(
        rotate_kernel,
        out_shape=jax.ShapeDtypeStruct((D, rows), BF),
        grid=(D // STRIP,),
        in_specs=[
            pl.BlockSpec(parts.shape, lambda i: (0, 0, 0)),
            pl.BlockSpec((1, D, STRIP), lambda i: (0, 0, i)),
        ]
        + [pl.BlockSpec(memory_space=pl.ANY)] * len(gates),
        out_specs=pl.BlockSpec((STRIP, rows), lambda i: (i, 0)),
        scratch_shapes=[pltpu.VMEM((rows, D), BF)],
        compiler_params=params(50),
        cost_estimate=pl.CostEstimate(
            flops=2 * rows * D * D, bytes_accessed=2 * D * D + 4 * rows * D, transcendentals=0
        ),
    )(parts, basis_in, *gates)


def encode(values, out_ref):
    most = jnp.max(values, axis=0, keepdims=True)
    power = jnp.clip(jnp.ceil(jnp.log2(jnp.maximum(most, 1e-37))), -126.0, 126.0)
    scaled = (values * jnp.exp2(-power)) * 65535.0 + 0.5
    code = jnp.minimum(scaled.astype(I32), 65535) - 32768
    out_ref[0:HALF, :] = code.astype(jnp.int16)
    out_ref[HALF:CODE_ROWS, :] = jnp.broadcast_to(power.astype(I32), (16, FF)).astype(jnp.int16)


def decode(code_ref):
    power = code_ref[HALF:CODE_ROWS, :].astype(I32)[0:1, :].astype(F32)
    value = (code_ref[0:HALF, :].astype(I32) + 32768).astype(F32)
    return value * (jnp.exp2(power) * (1.0 / 65535.0))


CODE = jax.ShapeDtypeStruct((CODE_ROWS, FF), jnp.int16)
BLOCK = jax.ShapeDtypeStruct((HALF, FF), F32)


N_FIRST = len(FIRST) * TOK
N_EARLY = ROWS - TOK


def block_sum(a_refs, g_refs, quarter, half):
    start = pl.multiple_of(quarter * QUARTER + half * HALF, HALF)
    first, second = a_refs
    early, last = g_refs
    middle = N_EARLY - N_FIRST
    total = jnp.dot(
        first[pl.ds(start, HALF), :], early[0:N_FIRST, :], preferred_element_type=F32
    )
    total += jnp.dot(
        second[pl.ds(start, HALF), 0:middle], early[N_FIRST:, :], preferred_element_type=F32
    )
    return total + jnp.dot(
        second[pl.ds(start, HALF), middle:], last[...], preferred_element_type=F32
    )


def early_kernel(*refs):
    rows_refs, (basis_ref, g_ref) = refs[:-2], refs[-2:]
    for k, rows_ref in enumerate(rows_refs):
        rotated = jnp.dot(rows_ref[...], basis_ref[0], preferred_element_type=F32)
        g_ref[k * TOK : (k + 1) * TOK, :] = (rotated * rotated).astype(BF)


def early_blocks(rows, basis_out):
    n = len(rows) * TOK
    return pl.pallas_call(
        early_kernel,
        out_shape=jax.ShapeDtypeStruct((n, FF), BF),
        in_specs=[IN_VMEM] * (len(rows) + 1),
        out_specs=IN_VMEM,
        compiler_params=params(8),
        cost_estimate=pl.CostEstimate(
            flops=2 * n * FF * FF, bytes_accessed=4 << 20, transcendentals=0
        ),
    )(*rows, basis_out)


def far_kernel(place_ref, rows_ref, basis_ref, first, second, early, last, up_ref, down_ref):
    rotated = jnp.dot(rows_ref[...], basis_ref[0], preferred_element_type=F32)
    last[...] = (rotated * rotated).astype(BF)
    encode(block_sum((first, second), (early, last), place_ref[0], 0), up_ref)
    encode(block_sum((first, second), (early, last), place_ref[0], 1), down_ref)


def far_blocks(place, rows, basis_out, a_sq, early):
    return pl.pallas_call(
        far_kernel,
        out_shape=(jax.ShapeDtypeStruct((TOK, FF), BF), CODE, CODE),
        in_specs=[IN_SMEM] + [IN_VMEM] * 5,
        out_specs=[IN_VMEM] * 3,
        compiler_params=params(8),
        cost_estimate=pl.CostEstimate(
            flops=2 * ROWS * FF * QUARTER, bytes_accessed=8 << 20, transcendentals=0
        ),
    )(place, rows, basis_out, *a_sq, early)


def near_kernel(place_ref, first, second, early, last, up_ref, down_ref):
    encode(block_sum((first, second), (early, last), place_ref[1], 1), up_ref)
    encode(block_sum((first, second), (early, last), place_ref[2], 0), down_ref)


def near_blocks(place, a_sq, g_sq):
    return pl.pallas_call(
        near_kernel,
        out_shape=(CODE, CODE),
        in_specs=[IN_SMEM] + [IN_VMEM] * 4,
        out_specs=[IN_VMEM] * 2,
        compiler_params=params(4),
        cost_estimate=pl.CostEstimate(
            flops=2 * ROWS * FF * QUARTER, bytes_accessed=4 << 20, transcendentals=0
        ),
    )(place, *a_sq, *g_sq)


def rest_kernel(place_ref, first, second, early, last, up_ref, down_ref, own_ref):
    a_refs, g_refs = (first, second), (early, last)
    up_ref[...] = block_sum(a_refs, g_refs, place_ref[1], 0)
    down_ref[...] = block_sum(a_refs, g_refs, place_ref[2], 1)
    own_ref[0:HALF, :] = block_sum(a_refs, g_refs, place_ref[3], 0)
    own_ref[HALF:QUARTER, :] = block_sum(a_refs, g_refs, place_ref[3], 1)


def rest_blocks(place, a_sq, g_sq):
    return pl.pallas_call(
        rest_kernel,
        out_shape=(BLOCK, BLOCK, jax.ShapeDtypeStruct((QUARTER, FF), F32)),
        in_specs=[IN_SMEM] + [IN_VMEM] * 4,
        out_specs=[IN_VMEM] * 3,
        compiler_params=params(4),
        cost_estimate=pl.CostEstimate(
            flops=4 * ROWS * FF * QUARTER, bytes_accessed=8 << 20, transcendentals=0
        ),
    )(place, *a_sq, *g_sq)


def pass_on_kernel(up_ref, down_ref, got_up_ref, got_down_ref, out_up_ref, out_down_ref):
    encode(up_ref[...] + decode(got_up_ref), out_up_ref)
    encode(down_ref[...] + decode(got_down_ref), out_down_ref)


def pass_on(up, down, got_up, got_down):
    return pl.pallas_call(
        pass_on_kernel,
        out_shape=(CODE, CODE),
        in_specs=[IN_VMEM] * 4,
        out_specs=[IN_VMEM] * 2,
        compiler_params=params(4),
    )(up, down, got_up, got_down)


LANES = 128
SPLIT = FF // LANES


def finish_kernel(own_ref, top_a_ref, top_b_ref, bottom_a_ref, bottom_b_ref, out_ref):
    top = own_ref[0:HALF, :] + decode(top_a_ref) + decode(top_b_ref)
    bottom = own_ref[HALF:QUARTER, :] + decode(bottom_a_ref) + decode(bottom_b_ref)
    for k in range(SPLIT):
        lanes = slice(k * LANES, (k + 1) * LANES)
        out_ref[pl.ds(k, HALF, stride=SPLIT), :] = top[:, lanes]
        out_ref[pl.ds(HALF * SPLIT + k, HALF, stride=SPLIT), :] = bottom[:, lanes]


def finish(own, top_a, top_b, bottom_a, bottom_b):
    return pl.pallas_call(
        finish_kernel,
        out_shape=jax.ShapeDtypeStruct((QUARTER * SPLIT, LANES), F32),
        in_specs=[IN_VMEM] * 5,
        out_specs=IN_VMEM,
        compiler_params=params(4),
    )(own, top_a, top_b, bottom_a, bottom_b)


def shift(value, axis, by):
    n = lax.axis_size(axis)
    return lax.ppermute(value, axis, [(i, (i + by) % n) for i in range(n)])


def to_owners(value):
    return lax.all_to_all(value, ("y", "c"), split_axis=0, concat_axis=0, tiled=True)


def z_ring(left, right):
    up, down = {0: (left, right)}, {0: (left, right)}
    for step in (1, 2, 3):
        up[step] = tuple(shift(v, "z", 1) for v in up[step - 1])
        down[step] = tuple(shift(v, "z", -1) for v in down[step - 1])
    ring = {**up, **{N_Z - step: down[step] for step in (1, 2, 3)}}
    ring[4] = (shift(up[3][0], "z", 1), shift(down[3][1], "z", -1))
    return ring


def on_device(tokens, grads, routing, basis_in, basis_out):
    x, z = lax.axis_index("x"), lax.axis_index("z")
    place = jnp.stack([x ^ 2, (x + 1) & 3, (x + 3) & 3, x]).astype(I32)
    here = z.astype(I32).reshape(1)

    ring = z_ring(*stage(tokens, routing.T))
    packed = pack_grads(here, routing.T, grads.reshape(TOK * TOP, FF), [])
    grads_in = to_owners(packed)
    by_z = regroup(grads_in, [*ring[3], *ring[5]])
    rows_out = [by_z[k] if k == 0 else shift(by_z[k], "z", k) for k in ORDER]

    in_order, gates = [], [grads_in, *ring[3], *ring[5]]
    for senders in (FIRST, SECOND):
        packed = pack_tokens(
            here, [ring[k][0] for k in senders], [ring[k][1] for k in senders], gates
        )
        gates = [packed] + [rows_out[ORDER.index(k)] for k in (1, 7, 2, 6, 3, 5)]
        in_order.append(to_owners(packed))
    early = early_blocks(rows_out[:-1], basis_out)
    a_sq = [rotate_inputs(in_order[0], basis_in, [])]
    a_sq.append(rotate_inputs(in_order[1], basis_in, [*a_sq, early]))

    last, far_up, far_down = far_blocks(place, rows_out[-1], basis_out, a_sq, early)
    g_sq = (early, last)
    got_far_up, got_far_down = shift(far_up, "x", 1), shift(far_down, "x", -1)
    near_up, near_down = near_blocks(place, a_sq, g_sq)
    got_near_up, got_near_down = shift(near_up, "x", 1), shift(near_down, "x", -1)
    up, down, own = rest_blocks(place, a_sq, g_sq)
    up, down = pass_on(up, down, got_far_up, got_far_down)
    got_up, got_down = shift(up, "x", 1), shift(down, "x", -1)
    values = finish(own, got_up, got_near_down, got_near_up, got_down)
    return values.reshape(QUARTER, 1, FF)


def solution(mesh):
    split = Mesh(mesh.devices.reshape(N_X, N_Z, N_Y, N_C), ("x", "z", "y", "c"))
    owner = ("z", "y", "c")
    everywhere = ("x", "z", "y", "c")
    return jax.shard_map(
        on_device,
        mesh=split,
        in_specs=(
            P(everywhere, None),
            P(everywhere, None, None),
            P(everywhere, None),
            P(owner, None, None),
            P(owner, None, None),
        ),
        out_specs=P("x", owner, None),
        check_vma=False,
    )
```

```python
import functools

import jax
import jax.numpy as jnp
from jax import lax
from jax.experimental import pallas as pl
from jax.experimental.pallas import tpu as pltpu
from jax.sharding import Mesh
from jax.sharding import PartitionSpec as P

CAP = 16
N_X, N_Z, N_Y, N_C = 4, 8, 4, 2
N_YC = N_Y * N_C
ORDER = (0, 1, 7, 2, 6, 3, 5, 4)
TOK = 128
TOP = 8
D = 2048
WIDE = D // 2
FF = 768
EXPERTS = 64
ROWS = EXPERTS * CAP
QUARTER = D // N_X
HALF = QUARTER // 2
CODE_ROWS = HALF + 16
BF = jnp.bfloat16
F32 = jnp.float32
I32 = jnp.int32
MIB = 1024 * 1024
IN_SMEM = pl.BlockSpec(memory_space=pltpu.SMEM)
IN_VMEM = pl.BlockSpec(memory_space=pltpu.VMEM)


def iota(shape, dim):
    return lax.broadcasted_iota(I32, shape, dim)


def params(mib):
    return pltpu.CompilerParams(vmem_limit_bytes=mib * MIB)


def ones_where(mask):
    return jnp.where(mask, 1.0, 0.0).astype(BF)


def earlier(n):
    return ones_where(iota((n, n), 0) < iota((n, n), 1))


def stage_kernel(tokens_ref, routing_ref, left_ref, right_ref):
    left_ref[0:TOK, :] = tokens_ref[:, 0:WIDE]
    left_ref[TOK:, :] = jnp.zeros((TOP, WIDE), BF)
    left_ref[TOK:, 0:TOK] = routing_ref[...].astype(F32).astype(BF)
    right_ref[...] = tokens_ref[:, WIDE:]


def stage(tokens, routing):
    return pl.pallas_call(
        stage_kernel,
        out_shape=(
            jax.ShapeDtypeStruct((TOK + TOP, WIDE), BF),
            jax.ShapeDtypeStruct((TOK, WIDE), BF),
        ),
        compiler_params=params(60),
    )(tokens, routing)


def pack_grads_kernel(here_ref, routing_ref, grads_ref, *refs):
    out_ref = refs[-1]
    pairs = TOK * TOP
    token = ones_where(iota((TOK, pairs), 1) // TOP == iota((TOK, pairs), 0))
    spread = jnp.dot(routing_ref[...].astype(F32).astype(BF), token, preferred_element_type=F32)
    choice = iota((TOP, pairs), 1) % TOP == iota((TOP, pairs), 0)
    flat = jnp.sum(jnp.where(choice, spread, 0.0), axis=0, keepdims=True).astype(I32)
    hit = iota((EXPERTS, pairs), 0) == flat
    before = jnp.dot(ones_where(hit), earlier(pairs), preferred_element_type=F32)
    rank = jnp.sum(jnp.where(hit, before, 0.0), axis=0, keepdims=True).astype(I32)
    along_z = (flat // N_YC + N_Z - here_ref[0]) % N_Z
    slot = jnp.where(flat < EXPERTS, (flat % N_YC) * TOK + along_z * CAP + rank, -1)
    grads = grads_ref[...]
    for k in range(N_YC):
        pick = ones_where(iota((TOK, pairs), 0) + k * TOK == slot)
        out_ref[k] = jnp.dot(pick, grads, preferred_element_type=F32).astype(BF)


def pack_grads(here, routing, grads, gates):
    return pl.pallas_call(
        pack_grads_kernel,
        out_shape=jax.ShapeDtypeStruct((N_YC, N_Z * CAP, FF), BF),
        in_specs=[IN_SMEM] + [IN_VMEM] * 2 + [pl.BlockSpec(memory_space=pl.ANY)] * len(gates),
        out_specs=IN_VMEM,
        compiler_params=params(60),
        cost_estimate=pl.CostEstimate(
            flops=2 * ROWS * ROWS * FF, bytes_accessed=4 * ROWS * FF, transcendentals=0
        ),
    )(here, routing, grads, *gates)


def regroup_kernel(*refs):
    in_ref, out_refs = refs[0], refs[-N_Z:]
    for k, out_ref in enumerate(out_refs):
        for i in range(N_YC):
            out_ref[i * CAP : (i + 1) * CAP, :] = in_ref[i, k * CAP : (k + 1) * CAP, :]


def regroup(blocks, others):
    return pl.pallas_call(
        regroup_kernel,
        out_shape=[jax.ShapeDtypeStruct((N_YC * CAP, FF), BF)] * N_Z,
        in_specs=[IN_VMEM] + [pl.BlockSpec(memory_space=pl.ANY)] * len(others),
        out_specs=[IN_VMEM] * N_Z,
        compiler_params=params(60),
    )(blocks, *others)


def pack_tokens_kernel(n, here_ref, *refs):
    lefts, rights, out_ref = refs[:n], refs[n : 2 * n], refs[-1]
    expert = iota((N_YC, TOK), 0) + here_ref[0] * N_YC
    rank = iota((CAP, TOK), 0)
    ahead = earlier(TOK)
    for b, (left, right) in enumerate(zip(lefts, rights)):
        routing = left[TOK:, 0:TOK].astype(F32).astype(I32)
        member = jnp.zeros((N_YC, TOK), F32)
        for j in range(TOP):
            member += jnp.where(routing[j : j + 1, :] == expert, 1.0, 0.0)
        before = jnp.dot(member.astype(BF), ahead, preferred_element_type=F32)
        slot = jnp.where(member > 0, before, -1.0).astype(I32)
        pick = jnp.concatenate([ones_where(slot[k : k + 1, :] == rank) for k in range(N_YC)], axis=0)
        for at, rows_ref in ((0, left), (WIDE, right)):
            rows = jnp.dot(pick, rows_ref[0:TOK, :], preferred_element_type=F32).astype(BF)
            out_ref[:, b * CAP : (b + 1) * CAP, at : at + WIDE] = rows.reshape(N_YC, CAP, WIDE)


def pack_tokens(here, lefts, rights, gates):
    n = len(lefts)
    return pl.pallas_call(
        functools.partial(pack_tokens_kernel, n),
        out_shape=jax.ShapeDtypeStruct((N_YC, n * CAP, D), BF),
        in_specs=[IN_SMEM] + [IN_VMEM] * (2 * n) + [pl.BlockSpec(memory_space=pl.ANY)] * len(gates),
        out_specs=IN_VMEM,
        compiler_params=params(60),
        cost_estimate=pl.CostEstimate(
            flops=2 * n * TOK * TOK * D, bytes_accessed=4 * n * TOK * D, transcendentals=0
        ),
    )(here, *lefts, *rights, *gates)


STRIP = 512


def rotate_kernel(rows_ref, basis_ref, *refs):
    rows = rows_ref[...].reshape(ROWS, D)
    rotated = jnp.dot(rows, basis_ref[0], preferred_element_type=F32)
    refs[-1][...] = jnp.transpose((rotated * rotated).astype(BF))


def rotate_inputs(rows, basis_in, gates):
    return pl.pallas_call(
        rotate_kernel,
        out_shape=jax.ShapeDtypeStruct((D, ROWS), BF),
        grid=(D // STRIP,),
        in_specs=[IN_VMEM, pl.BlockSpec((1, D, STRIP), lambda i: (0, 0, i))]
        + [pl.BlockSpec(memory_space=pl.ANY)] * len(gates),
        out_specs=pl.BlockSpec((STRIP, ROWS), lambda i: (i, 0)),
        compiler_params=params(54),
        cost_estimate=pl.CostEstimate(
            flops=2 * ROWS * D * D, bytes_accessed=2 * D * D + 4 * ROWS * D, transcendentals=0
        ),
    )(rows, basis_in, *gates)


def encode(values, out_ref):
    most = jnp.max(values, axis=0, keepdims=True)
    power = jnp.clip(jnp.ceil(jnp.log2(jnp.maximum(most, 1e-37))), -126.0, 126.0)
    scaled = (values * jnp.exp2(-power)) * 65535.0 + 0.5
    code = jnp.minimum(scaled.astype(I32), 65535) - 32768
    out_ref[0:HALF, :] = code.astype(jnp.int16)
    out_ref[HALF:CODE_ROWS, :] = jnp.broadcast_to(power.astype(I32), (16, FF)).astype(jnp.int16)


def decode(code_ref):
    power = code_ref[HALF:CODE_ROWS, :].astype(I32)[0:1, :].astype(F32)
    value = (code_ref[0:HALF, :].astype(I32) + 32768).astype(F32)
    return value * (jnp.exp2(power) * (1.0 / 65535.0))


CODE = jax.ShapeDtypeStruct((CODE_ROWS, FF), jnp.int16)
BLOCK = jax.ShapeDtypeStruct((HALF, FF), F32)


def block_sum(a_ref, g_ref, quarter, half):
    start = pl.multiple_of(quarter * QUARTER + half * HALF, HALF)
    return jnp.dot(a_ref[pl.ds(start, HALF), :], g_ref[...], preferred_element_type=F32)


def rotate_grads_kernel(*refs):
    rows_refs, (basis_ref, g_ref) = refs[:-2], refs[-2:]
    for k, rows_ref in enumerate(rows_refs):
        rotated = jnp.dot(rows_ref[...], basis_ref[0], preferred_element_type=F32)
        squared = (rotated * rotated).astype(BF)
        for i in range(N_YC):
            start = i * TOK + k * CAP
            g_ref[start : start + CAP, :] = squared[i * CAP : (i + 1) * CAP, :]


def rotate_grads(rows, basis_out):
    return pl.pallas_call(
        rotate_grads_kernel,
        out_shape=jax.ShapeDtypeStruct((ROWS, FF), BF),
        in_specs=[IN_VMEM] * (N_Z + 1),
        out_specs=IN_VMEM,
        compiler_params=params(8),
        cost_estimate=pl.CostEstimate(
            flops=2 * ROWS * FF * FF, bytes_accessed=4 << 20, transcendentals=0
        ),
    )(*rows, basis_out)


def far_kernel(place_ref, a_ref, g_ref, up_ref, down_ref):
    encode(block_sum(a_ref, g_ref, place_ref[0], 0), up_ref)
    encode(block_sum(a_ref, g_ref, place_ref[0], 1), down_ref)


def far_blocks(place, a_sq, g_sq):
    return pl.pallas_call(
        far_kernel,
        out_shape=(CODE, CODE),
        in_specs=[IN_SMEM] + [IN_VMEM] * 2,
        out_specs=[IN_VMEM] * 2,
        compiler_params=params(4),
        cost_estimate=pl.CostEstimate(
            flops=2 * ROWS * FF * QUARTER, bytes_accessed=4 << 20, transcendentals=0
        ),
    )(place, a_sq, g_sq)


def near_kernel(place_ref, a_ref, g_ref, up_ref, down_ref):
    encode(block_sum(a_ref, g_ref, place_ref[1], 1), up_ref)
    encode(block_sum(a_ref, g_ref, place_ref[2], 0), down_ref)


def near_blocks(place, a_sq, g_sq):
    return pl.pallas_call(
        near_kernel,
        out_shape=(CODE, CODE),
        in_specs=[IN_SMEM] + [IN_VMEM] * 2,
        out_specs=[IN_VMEM] * 2,
        compiler_params=params(4),
        cost_estimate=pl.CostEstimate(
            flops=2 * ROWS * FF * QUARTER, bytes_accessed=4 << 20, transcendentals=0
        ),
    )(place, a_sq, g_sq)


def rest_kernel(place_ref, a_ref, g_ref, up_ref, down_ref, own_ref):
    up_ref[...] = block_sum(a_ref, g_ref, place_ref[1], 0)
    down_ref[...] = block_sum(a_ref, g_ref, place_ref[2], 1)
    own_ref[0:HALF, :] = block_sum(a_ref, g_ref, place_ref[3], 0)
    own_ref[HALF:QUARTER, :] = block_sum(a_ref, g_ref, place_ref[3], 1)


def rest_blocks(place, a_sq, g_sq):
    return pl.pallas_call(
        rest_kernel,
        out_shape=(BLOCK, BLOCK, jax.ShapeDtypeStruct((QUARTER, FF), F32)),
        in_specs=[IN_SMEM] + [IN_VMEM] * 2,
        out_specs=[IN_VMEM] * 3,
        compiler_params=params(4),
        cost_estimate=pl.CostEstimate(
            flops=4 * ROWS * FF * QUARTER, bytes_accessed=8 << 20, transcendentals=0
        ),
    )(place, a_sq, g_sq)


def pass_on_kernel(up_ref, down_ref, got_up_ref, got_down_ref, out_up_ref, out_down_ref):
    encode(up_ref[...] + decode(got_up_ref), out_up_ref)
    encode(down_ref[...] + decode(got_down_ref), out_down_ref)


def pass_on(up, down, got_up, got_down):
    return pl.pallas_call(
        pass_on_kernel,
        out_shape=(CODE, CODE),
        in_specs=[IN_VMEM] * 4,
        out_specs=[IN_VMEM] * 2,
        compiler_params=params(4),
    )(up, down, got_up, got_down)


LANES = 128
SPLIT = FF // LANES


def finish_kernel(own_ref, top_a_ref, top_b_ref, bottom_a_ref, bottom_b_ref, out_ref):
    top = own_ref[0:HALF, :] + decode(top_a_ref) + decode(top_b_ref)
    bottom = own_ref[HALF:QUARTER, :] + decode(bottom_a_ref) + decode(bottom_b_ref)
    for k in range(SPLIT):
        lanes = slice(k * LANES, (k + 1) * LANES)
        out_ref[pl.ds(k, HALF, stride=SPLIT), :] = top[:, lanes]
        out_ref[pl.ds(HALF * SPLIT + k, HALF, stride=SPLIT), :] = bottom[:, lanes]


def finish(own, top_a, top_b, bottom_a, bottom_b):
    return pl.pallas_call(
        finish_kernel,
        out_shape=jax.ShapeDtypeStruct((QUARTER * SPLIT, LANES), F32),
        in_specs=[IN_VMEM] * 5,
        out_specs=IN_VMEM,
        compiler_params=params(4),
    )(own, top_a, top_b, bottom_a, bottom_b)


def shift(value, axis, by):
    n = lax.axis_size(axis)
    return lax.ppermute(value, axis, [(i, (i + by) % n) for i in range(n)])


def to_owners(value):
    return lax.all_to_all(value, ("y", "c"), split_axis=0, concat_axis=0, tiled=True)


def z_ring(left, right):
    up, down = {0: (left, right)}, {0: (left, right)}
    for step in (1, 2, 3):
        up[step] = tuple(shift(v, "z", 1) for v in up[step - 1])
        down[step] = tuple(shift(v, "z", -1) for v in down[step - 1])
    ring = {**up, **{N_Z - step: down[step] for step in (1, 2, 3)}}
    ring[4] = (shift(up[3][0], "z", 1), shift(down[3][1], "z", -1))
    return ring


def on_device(tokens, grads, routing, basis_in, basis_out):
    x, z = lax.axis_index("x"), lax.axis_index("z")
    place = jnp.stack([x ^ 2, (x + 1) & 3, (x + 3) & 3, x]).astype(I32)
    here = z.astype(I32).reshape(1)

    ring = z_ring(*stage(tokens, routing.T))
    packed = pack_grads(here, routing.T, grads.reshape(TOK * TOP, FF), [])
    grads_in = to_owners(packed)
    by_z = regroup(grads_in, [*ring[3], *ring[5]])
    rows_out = [by_z[k] if k == 0 else shift(by_z[k], "z", k) for k in ORDER]

    rows_in = to_owners(
        pack_tokens(here, [ring[k][0] for k in ORDER], [ring[k][1] for k in ORDER], [grads_in])
    )
    g_sq = rotate_grads(rows_out, basis_out)
    a_sq = rotate_inputs(rows_in, basis_in, [g_sq])

    far_up, far_down = far_blocks(place, a_sq, g_sq)
    got_far_up, got_far_down = shift(far_up, "x", 1), shift(far_down, "x", -1)
    near_up, near_down = near_blocks(place, a_sq, g_sq)
    got_near_up, got_near_down = shift(near_up, "x", 1), shift(near_down, "x", -1)
    up, down, own = rest_blocks(place, a_sq, g_sq)
    up, down = pass_on(up, down, got_far_up, got_far_down)
    got_up, got_down = shift(up, "x", 1), shift(down, "x", -1)
    values = finish(own, got_up, got_near_down, got_near_up, got_down)
    return values.reshape(QUARTER, 1, FF)


def solution(mesh):
    split = Mesh(mesh.devices.reshape(N_X, N_Z, N_Y, N_C), ("x", "z", "y", "c"))
    owner = ("z", "y", "c")
    everywhere = ("x", "z", "y", "c")
    return jax.shard_map(
        on_device,
        mesh=split,
        in_specs=(
            P(everywhere, None),
            P(everywhere, None, None),
            P(everywhere, None),
            P(owner, None, None),
            P(owner, None, None),
        ),
        out_specs=P("x", owner, None),
        check_vma=False,
    )
```

```python
import functools

import jax
import jax.numpy as jnp
from jax import lax
from jax.experimental import pallas as pl
from jax.experimental.pallas import tpu as pltpu
from jax.sharding import Mesh
from jax.sharding import PartitionSpec as P

CAP = 16
N_X, N_Z, N_Y, N_C = 4, 8, 4, 2
N_YC = N_Y * N_C
ORDER = (0, 1, 7, 2, 6, 3, 5, 4)
TOK = 128
TOP = 8
D = 2048
WIDE = D // 2
FF = 768
EXPERTS = 64
ROWS = EXPERTS * CAP
QUARTER = D // N_X
HALF = QUARTER // 2
CODE_ROWS = HALF + 16
BF = jnp.bfloat16
F32 = jnp.float32
I32 = jnp.int32
MIB = 1024 * 1024
IN_SMEM = pl.BlockSpec(memory_space=pltpu.SMEM)
IN_VMEM = pl.BlockSpec(memory_space=pltpu.VMEM)


def iota(shape, dim):
    return lax.broadcasted_iota(I32, shape, dim)


def params(mib):
    return pltpu.CompilerParams(vmem_limit_bytes=mib * MIB)


def ones_where(mask):
    return jnp.where(mask, 1.0, 0.0).astype(BF)


def earlier(n):
    return ones_where(iota((n, n), 0) < iota((n, n), 1))


def stage_kernel(tokens_ref, routing_ref, left_ref, right_ref):
    left_ref[0:TOK, :] = tokens_ref[:, 0:WIDE]
    left_ref[TOK:, :] = jnp.zeros((TOP, WIDE), BF)
    left_ref[TOK:, 0:TOK] = routing_ref[...].astype(F32).astype(BF)
    right_ref[...] = tokens_ref[:, WIDE:]


def stage(tokens, routing):
    return pl.pallas_call(
        stage_kernel,
        out_shape=(
            jax.ShapeDtypeStruct((TOK + TOP, WIDE), BF),
            jax.ShapeDtypeStruct((TOK, WIDE), BF),
        ),
        compiler_params=params(60),
    )(tokens, routing)


def pack_grads_kernel(here_ref, routing_ref, grads_ref, *refs):
    out_ref = refs[-1]
    pairs = TOK * TOP
    token = ones_where(iota((TOK, pairs), 1) // TOP == iota((TOK, pairs), 0))
    spread = jnp.dot(routing_ref[...].astype(F32).astype(BF), token, preferred_element_type=F32)
    choice = iota((TOP, pairs), 1) % TOP == iota((TOP, pairs), 0)
    flat = jnp.sum(jnp.where(choice, spread, 0.0), axis=0, keepdims=True).astype(I32)
    hit = iota((EXPERTS, pairs), 0) == flat
    before = jnp.dot(ones_where(hit), earlier(pairs), preferred_element_type=F32)
    rank = jnp.sum(jnp.where(hit, before, 0.0), axis=0, keepdims=True).astype(I32)
    along_z = (flat // N_YC + N_Z - here_ref[0]) % N_Z
    slot = jnp.where(flat < EXPERTS, (flat % N_YC) * TOK + along_z * CAP + rank, -1)
    grads = grads_ref[...]
    for k in range(N_YC):
        pick = ones_where(iota((TOK, pairs), 0) + k * TOK == slot)
        out_ref[k] = jnp.dot(pick, grads, preferred_element_type=F32).astype(BF)


def pack_grads(here, routing, grads, gates):
    return pl.pallas_call(
        pack_grads_kernel,
        out_shape=jax.ShapeDtypeStruct((N_YC, N_Z * CAP, FF), BF),
        in_specs=[IN_SMEM] + [IN_VMEM] * 2 + [pl.BlockSpec(memory_space=pl.ANY)] * len(gates),
        out_specs=IN_VMEM,
        compiler_params=params(60),
        cost_estimate=pl.CostEstimate(
            flops=2 * ROWS * ROWS * FF, bytes_accessed=4 * ROWS * FF, transcendentals=0
        ),
    )(here, routing, grads, *gates)


def regroup_kernel(*refs):
    in_ref, out_refs = refs[0], refs[-N_Z:]
    for k, out_ref in enumerate(out_refs):
        for i in range(N_YC):
            out_ref[i * CAP : (i + 1) * CAP, :] = in_ref[i, k * CAP : (k + 1) * CAP, :]


def regroup(blocks, others):
    return pl.pallas_call(
        regroup_kernel,
        out_shape=[jax.ShapeDtypeStruct((N_YC * CAP, FF), BF)] * N_Z,
        in_specs=[IN_VMEM] + [pl.BlockSpec(memory_space=pl.ANY)] * len(others),
        out_specs=[IN_VMEM] * N_Z,
        compiler_params=params(60),
    )(blocks, *others)


def pack_tokens_kernel(n, here_ref, *refs):
    lefts, rights, out_ref = refs[:n], refs[n : 2 * n], refs[-1]
    expert = iota((N_YC, TOK), 0) + here_ref[0] * N_YC
    rank = iota((CAP, TOK), 0)
    ahead = earlier(TOK)
    for b, (left, right) in enumerate(zip(lefts, rights)):
        routing = left[TOK:, 0:TOK].astype(F32).astype(I32)
        member = jnp.zeros((N_YC, TOK), F32)
        for j in range(TOP):
            member += jnp.where(routing[j : j + 1, :] == expert, 1.0, 0.0)
        before = jnp.dot(member.astype(BF), ahead, preferred_element_type=F32)
        slot = jnp.where(member > 0, before, -1.0).astype(I32)
        pick = jnp.concatenate([ones_where(slot[k : k + 1, :] == rank) for k in range(N_YC)], axis=0)
        for at, rows_ref in ((0, left), (WIDE, right)):
            rows = jnp.dot(pick, rows_ref[0:TOK, :], preferred_element_type=F32).astype(BF)
            out_ref[:, b * CAP : (b + 1) * CAP, at : at + WIDE] = rows.reshape(N_YC, CAP, WIDE)


def pack_tokens(here, lefts, rights, gates):
    n = len(lefts)
    return pl.pallas_call(
        functools.partial(pack_tokens_kernel, n),
        out_shape=jax.ShapeDtypeStruct((N_YC, n * CAP, D), BF),
        in_specs=[IN_SMEM] + [IN_VMEM] * (2 * n) + [pl.BlockSpec(memory_space=pl.ANY)] * len(gates),
        out_specs=IN_VMEM,
        compiler_params=params(60),
        cost_estimate=pl.CostEstimate(
            flops=2 * n * TOK * TOK * D, bytes_accessed=4 * n * TOK * D, transcendentals=0
        ),
    )(here, *lefts, *rights, *gates)


STRIP = 512


def rotate_kernel(rows_ref, basis_ref, *refs):
    rows = rows_ref[...].reshape(ROWS, D)
    rotated = jnp.dot(rows, basis_ref[0], preferred_element_type=F32)
    refs[-1][...] = jnp.transpose((rotated * rotated).astype(BF))


def rotate_inputs(rows, basis_in, gates):
    return pl.pallas_call(
        rotate_kernel,
        out_shape=jax.ShapeDtypeStruct((D, ROWS), BF),
        grid=(D // STRIP,),
        in_specs=[IN_VMEM, pl.BlockSpec((1, D, STRIP), lambda i: (0, 0, i))]
        + [pl.BlockSpec(memory_space=pl.ANY)] * len(gates),
        out_specs=pl.BlockSpec((STRIP, ROWS), lambda i: (i, 0)),
        compiler_params=params(46),
        cost_estimate=pl.CostEstimate(
            flops=2 * ROWS * D * D, bytes_accessed=2 * D * D + 4 * ROWS * D, transcendentals=0
        ),
    )(rows, basis_in, *gates)


def encode(values, out_ref):
    most = jnp.max(values, axis=0, keepdims=True)
    power = jnp.clip(jnp.ceil(jnp.log2(jnp.maximum(most, 1e-37))), -126.0, 126.0)
    scaled = (values * jnp.exp2(-power)) * 65535.0 + 0.5
    code = jnp.minimum(scaled.astype(I32), 65535) - 32768
    out_ref[0:HALF, :] = code.astype(jnp.int16)
    out_ref[HALF:CODE_ROWS, :] = jnp.broadcast_to(power.astype(I32), (16, FF)).astype(jnp.int16)


def decode(code_ref):
    power = code_ref[HALF:CODE_ROWS, :].astype(I32)[0:1, :].astype(F32)
    value = (code_ref[0:HALF, :].astype(I32) + 32768).astype(F32)
    return value * (jnp.exp2(power) * (1.0 / 65535.0))


CODE = jax.ShapeDtypeStruct((CODE_ROWS, FF), jnp.int16)
BLOCK = jax.ShapeDtypeStruct((HALF, FF), F32)


def block_sum(a_ref, g_ref, quarter, half):
    start = pl.multiple_of(quarter * QUARTER + half * HALF, HALF)
    return jnp.dot(a_ref[pl.ds(start, HALF), :], g_ref[...], preferred_element_type=F32)


def rotate_grads_kernel(*refs):
    rows_refs, (basis_ref, g_ref) = refs[:-2], refs[-2:]
    for k, rows_ref in enumerate(rows_refs):
        rotated = jnp.dot(rows_ref[...], basis_ref[0], preferred_element_type=F32)
        squared = (rotated * rotated).astype(BF)
        for i in range(N_YC):
            start = i * TOK + k * CAP
            g_ref[start : start + CAP, :] = squared[i * CAP : (i + 1) * CAP, :]


def rotate_grads(rows, basis_out):
    return pl.pallas_call(
        rotate_grads_kernel,
        out_shape=jax.ShapeDtypeStruct((ROWS, FF), BF),
        in_specs=[IN_VMEM] * (N_Z + 1),
        out_specs=IN_VMEM,
        compiler_params=params(8),
        cost_estimate=pl.CostEstimate(
            flops=2 * ROWS * FF * FF, bytes_accessed=4 << 20, transcendentals=0
        ),
    )(*rows, basis_out)


def far_kernel(place_ref, a_ref, g_ref, up_ref, down_ref):
    encode(block_sum(a_ref, g_ref, place_ref[0], 0), up_ref)
    encode(block_sum(a_ref, g_ref, place_ref[0], 1), down_ref)


def far_blocks(place, a_sq, g_sq):
    return pl.pallas_call(
        far_kernel,
        out_shape=(CODE, CODE),
        in_specs=[IN_SMEM] + [IN_VMEM] * 2,
        out_specs=[IN_VMEM] * 2,
        compiler_params=params(4),
        cost_estimate=pl.CostEstimate(
            flops=2 * ROWS * FF * QUARTER, bytes_accessed=4 << 20, transcendentals=0
        ),
    )(place, a_sq, g_sq)


def near_kernel(place_ref, a_ref, g_ref, up_ref, down_ref):
    encode(block_sum(a_ref, g_ref, place_ref[1], 1), up_ref)
    encode(block_sum(a_ref, g_ref, place_ref[2], 0), down_ref)


def near_blocks(place, a_sq, g_sq):
    return pl.pallas_call(
        near_kernel,
        out_shape=(CODE, CODE),
        in_specs=[IN_SMEM] + [IN_VMEM] * 2,
        out_specs=[IN_VMEM] * 2,
        compiler_params=params(4),
        cost_estimate=pl.CostEstimate(
            flops=2 * ROWS * FF * QUARTER, bytes_accessed=4 << 20, transcendentals=0
        ),
    )(place, a_sq, g_sq)


def rest_kernel(place_ref, a_ref, g_ref, up_ref, down_ref, own_ref):
    up_ref[...] = block_sum(a_ref, g_ref, place_ref[1], 0)
    down_ref[...] = block_sum(a_ref, g_ref, place_ref[2], 1)
    own_ref[0:HALF, :] = block_sum(a_ref, g_ref, place_ref[3], 0)
    own_ref[HALF:QUARTER, :] = block_sum(a_ref, g_ref, place_ref[3], 1)


def rest_blocks(place, a_sq, g_sq):
    return pl.pallas_call(
        rest_kernel,
        out_shape=(BLOCK, BLOCK, jax.ShapeDtypeStruct((QUARTER, FF), F32)),
        in_specs=[IN_SMEM] + [IN_VMEM] * 2,
        out_specs=[IN_VMEM] * 3,
        compiler_params=params(4),
        cost_estimate=pl.CostEstimate(
            flops=4 * ROWS * FF * QUARTER, bytes_accessed=8 << 20, transcendentals=0
        ),
    )(place, a_sq, g_sq)


def pass_on_kernel(up_ref, down_ref, got_up_ref, got_down_ref, out_up_ref, out_down_ref):
    encode(up_ref[...] + decode(got_up_ref), out_up_ref)
    encode(down_ref[...] + decode(got_down_ref), out_down_ref)


def pass_on(up, down, got_up, got_down):
    return pl.pallas_call(
        pass_on_kernel,
        out_shape=(CODE, CODE),
        in_specs=[IN_VMEM] * 4,
        out_specs=[IN_VMEM] * 2,
        compiler_params=params(4),
    )(up, down, got_up, got_down)


LANES = 128
SPLIT = FF // LANES


def finish_kernel(own_ref, top_a_ref, top_b_ref, bottom_a_ref, bottom_b_ref, out_ref):
    top = own_ref[0:HALF, :] + decode(top_a_ref) + decode(top_b_ref)
    bottom = own_ref[HALF:QUARTER, :] + decode(bottom_a_ref) + decode(bottom_b_ref)
    for k in range(SPLIT):
        lanes = slice(k * LANES, (k + 1) * LANES)
        out_ref[pl.ds(k, HALF, stride=SPLIT), :] = top[:, lanes]
        out_ref[pl.ds(HALF * SPLIT + k, HALF, stride=SPLIT), :] = bottom[:, lanes]


def finish(own, top_a, top_b, bottom_a, bottom_b):
    return pl.pallas_call(
        finish_kernel,
        out_shape=jax.ShapeDtypeStruct((QUARTER * SPLIT, LANES), F32),
        in_specs=[IN_VMEM] * 5,
        out_specs=IN_VMEM,
        compiler_params=params(4),
    )(own, top_a, top_b, bottom_a, bottom_b)


def shift(value, axis, by):
    n = lax.axis_size(axis)
    return lax.ppermute(value, axis, [(i, (i + by) % n) for i in range(n)])


def to_owners(value):
    return lax.all_to_all(value, ("y", "c"), split_axis=0, concat_axis=0, tiled=True)


def z_ring(left, right):
    up, down = {0: (left, right)}, {0: (left, right)}
    for step in (1, 2, 3):
        up[step] = tuple(shift(v, "z", 1) for v in up[step - 1])
        down[step] = tuple(shift(v, "z", -1) for v in down[step - 1])
    ring = {**up, **{N_Z - step: down[step] for step in (1, 2, 3)}}
    ring[4] = (shift(up[3][0], "z", 1), shift(down[3][1], "z", -1))
    return ring


def on_device(tokens, grads, routing, basis_in, basis_out):
    x, z = lax.axis_index("x"), lax.axis_index("z")
    place = jnp.stack([x ^ 2, (x + 1) & 3, (x + 3) & 3, x]).astype(I32)
    here = z.astype(I32).reshape(1)

    ring = z_ring(*stage(tokens, routing.T))
    packed = pack_grads(here, routing.T, grads.reshape(TOK * TOP, FF), [ring[2][0], ring[2][1], ring[6][0], ring[6][1]])
    grads_in = to_owners(packed)
    by_z = regroup(grads_in, [*ring[3], *ring[5]])
    rows_out = [by_z[k] if k == 0 else shift(by_z[k], "z", k) for k in ORDER]

    rows_in = to_owners(
        pack_tokens(here, [ring[k][0] for k in ORDER], [ring[k][1] for k in ORDER], [grads_in])
    )
    g_sq = rotate_grads(rows_out, basis_out)
    a_sq = rotate_inputs(rows_in, basis_in, [g_sq])

    far_up, far_down = far_blocks(place, a_sq, g_sq)
    got_far_up, got_far_down = shift(far_up, "x", 1), shift(far_down, "x", -1)
    near_up, near_down = near_blocks(place, a_sq, g_sq)
    got_near_up, got_near_down = shift(near_up, "x", 1), shift(near_down, "x", -1)
    up, down, own = rest_blocks(place, a_sq, g_sq)
    up, down = pass_on(up, down, got_far_up, got_far_down)
    got_up, got_down = shift(up, "x", 1), shift(down, "x", -1)
    values = finish(own, got_up, got_near_down, got_near_up, got_down)
    return values.reshape(QUARTER, 1, FF)


def solution(mesh):
    split = Mesh(mesh.devices.reshape(N_X, N_Z, N_Y, N_C), ("x", "z", "y", "c"))
    owner = ("z", "y", "c")
    everywhere = ("x", "z", "y", "c")
    return jax.shard_map(
        on_device,
        mesh=split,
        in_specs=(
            P(everywhere, None),
            P(everywhere, None, None),
            P(everywhere, None),
            P(owner, None, None),
            P(owner, None, None),
        ),
        out_specs=P("x", owner, None),
        check_vma=False,
    )
```

```python
import functools

import jax
import jax.numpy as jnp
from jax import lax
from jax.experimental import pallas as pl
from jax.experimental.pallas import tpu as pltpu
from jax.sharding import Mesh
from jax.sharding import PartitionSpec as P

CAP = 16
N_X, N_Z, N_Y, N_C = 4, 8, 4, 2
N_YC = N_Y * N_C
ORDER = (0, 1, 7, 2, 6, 3, 5, 4)
TOK = 128
TOP = 8
D = 2048
WIDE = D // 2
FF = 768
EXPERTS = 64
ROWS = EXPERTS * CAP
QUARTER = D // N_X
HALF = QUARTER // 2
CODE_ROWS = HALF + 16
BF = jnp.bfloat16
F32 = jnp.float32
I32 = jnp.int32
MIB = 1024 * 1024
IN_SMEM = pl.BlockSpec(memory_space=pltpu.SMEM)
IN_VMEM = pl.BlockSpec(memory_space=pltpu.VMEM)


def iota(shape, dim):
    return lax.broadcasted_iota(I32, shape, dim)


def params(mib):
    return pltpu.CompilerParams(vmem_limit_bytes=mib * MIB)


def ones_where(mask):
    return jnp.where(mask, 1.0, 0.0).astype(BF)


def earlier(n):
    return ones_where(iota((n, n), 0) < iota((n, n), 1))


def stage_kernel(tokens_ref, routing_ref, left_ref, right_ref):
    left_ref[0:TOK, :] = tokens_ref[:, 0:WIDE]
    left_ref[TOK:, :] = jnp.zeros((TOP, WIDE), BF)
    left_ref[TOK:, 0:TOK] = routing_ref[...].astype(F32).astype(BF)
    right_ref[...] = tokens_ref[:, WIDE:]


def stage(tokens, routing):
    return pl.pallas_call(
        stage_kernel,
        out_shape=(
            jax.ShapeDtypeStruct((TOK + TOP, WIDE), BF),
            jax.ShapeDtypeStruct((TOK, WIDE), BF),
        ),
        compiler_params=params(60),
    )(tokens, routing)


def pack_grads_kernel(here_ref, routing_ref, grads_ref, *refs):
    out_ref = refs[-1]
    pairs = TOK * TOP
    token = ones_where(iota((TOK, pairs), 1) // TOP == iota((TOK, pairs), 0))
    spread = jnp.dot(routing_ref[...].astype(F32).astype(BF), token, preferred_element_type=F32)
    choice = iota((TOP, pairs), 1) % TOP == iota((TOP, pairs), 0)
    flat = jnp.sum(jnp.where(choice, spread, 0.0), axis=0, keepdims=True).astype(I32)
    hit = iota((EXPERTS, pairs), 0) == flat
    before = jnp.dot(ones_where(hit), earlier(pairs), preferred_element_type=F32)
    rank = jnp.sum(jnp.where(hit, before, 0.0), axis=0, keepdims=True).astype(I32)
    along_z = (flat // N_YC + N_Z - here_ref[0]) % N_Z
    slot = jnp.where(flat < EXPERTS, (flat % N_YC) * TOK + along_z * CAP + rank, -1)
    grads = grads_ref[...]
    for k in range(N_YC):
        pick = ones_where(iota((TOK, pairs), 0) + k * TOK == slot)
        out_ref[k] = jnp.dot(pick, grads, preferred_element_type=F32).astype(BF)


def pack_grads(here, routing, grads, gates):
    return pl.pallas_call(
        pack_grads_kernel,
        out_shape=jax.ShapeDtypeStruct((N_YC, N_Z * CAP, FF), BF),
        in_specs=[IN_SMEM] + [IN_VMEM] * 2 + [pl.BlockSpec(memory_space=pl.ANY)] * len(gates),
        out_specs=IN_VMEM,
        compiler_params=params(60),
        cost_estimate=pl.CostEstimate(
            flops=2 * ROWS * ROWS * FF, bytes_accessed=4 * ROWS * FF, transcendentals=0
        ),
    )(here, routing, grads, *gates)


def regroup_kernel(*refs):
    in_ref, out_refs = refs[0], refs[-N_Z:]
    for k, out_ref in enumerate(out_refs):
        for i in range(N_YC):
            out_ref[i * CAP : (i + 1) * CAP, :] = in_ref[i, k * CAP : (k + 1) * CAP, :]


def regroup(blocks, others):
    return pl.pallas_call(
        regroup_kernel,
        out_shape=[jax.ShapeDtypeStruct((N_YC * CAP, FF), BF)] * N_Z,
        in_specs=[IN_VMEM] + [pl.BlockSpec(memory_space=pl.ANY)] * len(others),
        out_specs=[IN_VMEM] * N_Z,
        compiler_params=params(60),
    )(blocks, *others)


def pack_tokens_kernel(n, here_ref, *refs):
    lefts, rights, out_ref = refs[:n], refs[n : 2 * n], refs[-1]
    expert = iota((N_YC, TOK), 0) + here_ref[0] * N_YC
    rank = iota((CAP, TOK), 0)
    ahead = earlier(TOK)
    for b, (left, right) in enumerate(zip(lefts, rights)):
        routing = left[TOK:, 0:TOK].astype(F32).astype(I32)
        member = jnp.zeros((N_YC, TOK), F32)
        for j in range(TOP):
            member += jnp.where(routing[j : j + 1, :] == expert, 1.0, 0.0)
        before = jnp.dot(member.astype(BF), ahead, preferred_element_type=F32)
        slot = jnp.where(member > 0, before, -1.0).astype(I32)
        pick = jnp.concatenate([ones_where(slot[k : k + 1, :] == rank) for k in range(N_YC)], axis=0)
        for at, rows_ref in ((0, left), (WIDE, right)):
            rows = jnp.dot(pick, rows_ref[0:TOK, :], preferred_element_type=F32).astype(BF)
            out_ref[:, b * CAP : (b + 1) * CAP, at : at + WIDE] = rows.reshape(N_YC, CAP, WIDE)


def pack_tokens(here, lefts, rights, gates):
    n = len(lefts)
    return pl.pallas_call(
        functools.partial(pack_tokens_kernel, n),
        out_shape=jax.ShapeDtypeStruct((N_YC, n * CAP, D), BF),
        in_specs=[IN_SMEM] + [IN_VMEM] * (2 * n) + [pl.BlockSpec(memory_space=pl.ANY)] * len(gates),
        out_specs=IN_VMEM,
        compiler_params=params(60),
        cost_estimate=pl.CostEstimate(
            flops=2 * n * TOK * TOK * D, bytes_accessed=4 * n * TOK * D, transcendentals=0
        ),
    )(here, *lefts, *rights, *gates)


STRIP = 512


def rotate_kernel(rows_ref, basis_ref, *refs):
    rows = rows_ref[...].reshape(ROWS, D)
    rotated = jnp.dot(rows, basis_ref[0], preferred_element_type=F32)
    refs[-1][...] = jnp.transpose((rotated * rotated).astype(BF))


def rotate_inputs(rows, basis_in, gates):
    return pl.pallas_call(
        rotate_kernel,
        out_shape=jax.ShapeDtypeStruct((D, ROWS), BF),
        grid=(D // STRIP,),
        in_specs=[IN_VMEM, pl.BlockSpec((1, D, STRIP), lambda i: (0, 0, i))]
        + [pl.BlockSpec(memory_space=pl.ANY)] * len(gates),
        out_specs=pl.BlockSpec((STRIP, ROWS), lambda i: (i, 0)),
        compiler_params=params(46),
        cost_estimate=pl.CostEstimate(
            flops=2 * ROWS * D * D, bytes_accessed=2 * D * D + 4 * ROWS * D, transcendentals=0
        ),
    )(rows, basis_in, *gates)


def encode(values, out_ref):
    most = jnp.max(values, axis=0, keepdims=True)
    power = jnp.clip(jnp.ceil(jnp.log2(jnp.maximum(most, 1e-37))), -126.0, 126.0)
    scaled = (values * jnp.exp2(-power)) * 65535.0 + 0.5
    code = jnp.minimum(scaled.astype(I32), 65535) - 32768
    out_ref[0:HALF, :] = code.astype(jnp.int16)
    out_ref[HALF:CODE_ROWS, :] = jnp.broadcast_to(power.astype(I32), (16, FF)).astype(jnp.int16)


def decode(code_ref):
    power = code_ref[HALF:CODE_ROWS, :].astype(I32)[0:1, :].astype(F32)
    value = (code_ref[0:HALF, :].astype(I32) + 32768).astype(F32)
    return value * (jnp.exp2(power) * (1.0 / 65535.0))


CODE = jax.ShapeDtypeStruct((CODE_ROWS, FF), jnp.int16)
BLOCK = jax.ShapeDtypeStruct((HALF, FF), F32)


def block_sum(a_ref, g_ref, quarter, half):
    start = pl.multiple_of(quarter * QUARTER + half * HALF, HALF)
    return jnp.dot(a_ref[pl.ds(start, HALF), :], g_ref[...], preferred_element_type=F32)


def rotate_grads_kernel(*refs):
    rows_refs, (basis_ref, g_ref) = refs[:-2], refs[-2:]
    for k, rows_ref in enumerate(rows_refs):
        rotated = jnp.dot(rows_ref[...], basis_ref[0], preferred_element_type=F32)
        squared = (rotated * rotated).astype(BF)
        for i in range(N_YC):
            start = i * TOK + k * CAP
            g_ref[start : start + CAP, :] = squared[i * CAP : (i + 1) * CAP, :]


def rotate_grads(rows, basis_out):
    return pl.pallas_call(
        rotate_grads_kernel,
        out_shape=jax.ShapeDtypeStruct((ROWS, FF), BF),
        in_specs=[IN_VMEM] * (N_Z + 1),
        out_specs=IN_VMEM,
        compiler_params=params(8),
        cost_estimate=pl.CostEstimate(
            flops=2 * ROWS * FF * FF, bytes_accessed=4 << 20, transcendentals=0
        ),
    )(*rows, basis_out)


def far_kernel(place_ref, a_ref, g_ref, up_ref, down_ref):
    encode(block_sum(a_ref, g_ref, place_ref[0], 0), up_ref)
    encode(block_sum(a_ref, g_ref, place_ref[0], 1), down_ref)


def far_blocks(place, a_sq, g_sq):
    return pl.pallas_call(
        far_kernel,
        out_shape=(CODE, CODE),
        in_specs=[IN_SMEM] + [IN_VMEM] * 2,
        out_specs=[IN_VMEM] * 2,
        compiler_params=params(4),
        cost_estimate=pl.CostEstimate(
            flops=2 * ROWS * FF * QUARTER, bytes_accessed=4 << 20, transcendentals=0
        ),
    )(place, a_sq, g_sq)


def near_kernel(place_ref, a_ref, g_ref, up_ref, down_ref):
    encode(block_sum(a_ref, g_ref, place_ref[1], 1), up_ref)
    encode(block_sum(a_ref, g_ref, place_ref[2], 0), down_ref)


def near_blocks(place, a_sq, g_sq):
    return pl.pallas_call(
        near_kernel,
        out_shape=(CODE, CODE),
        in_specs=[IN_SMEM] + [IN_VMEM] * 2,
        out_specs=[IN_VMEM] * 2,
        compiler_params=params(4),
        cost_estimate=pl.CostEstimate(
            flops=2 * ROWS * FF * QUARTER, bytes_accessed=4 << 20, transcendentals=0
        ),
    )(place, a_sq, g_sq)


def rest_kernel(place_ref, a_ref, g_ref, up_ref, down_ref, own_ref):
    up_ref[...] = block_sum(a_ref, g_ref, place_ref[1], 0)
    down_ref[...] = block_sum(a_ref, g_ref, place_ref[2], 1)
    own_ref[0:HALF, :] = block_sum(a_ref, g_ref, place_ref[3], 0)
    own_ref[HALF:QUARTER, :] = block_sum(a_ref, g_ref, place_ref[3], 1)


def rest_blocks(place, a_sq, g_sq):
    return pl.pallas_call(
        rest_kernel,
        out_shape=(BLOCK, BLOCK, jax.ShapeDtypeStruct((QUARTER, FF), F32)),
        in_specs=[IN_SMEM] + [IN_VMEM] * 2,
        out_specs=[IN_VMEM] * 3,
        compiler_params=params(4),
        cost_estimate=pl.CostEstimate(
            flops=4 * ROWS * FF * QUARTER, bytes_accessed=8 << 20, transcendentals=0
        ),
    )(place, a_sq, g_sq)


def pass_on_kernel(up_ref, down_ref, got_up_ref, got_down_ref, out_up_ref, out_down_ref):
    encode(up_ref[...] + decode(got_up_ref), out_up_ref)
    encode(down_ref[...] + decode(got_down_ref), out_down_ref)


def pass_on(up, down, got_up, got_down):
    return pl.pallas_call(
        pass_on_kernel,
        out_shape=(CODE, CODE),
        in_specs=[IN_VMEM] * 4,
        out_specs=[IN_VMEM] * 2,
        compiler_params=params(4),
    )(up, down, got_up, got_down)


LANES = 128
SPLIT = FF // LANES


def finish_kernel(own_ref, top_a_ref, top_b_ref, bottom_a_ref, bottom_b_ref, out_ref):
    top = own_ref[0:HALF, :] + decode(top_a_ref) + decode(top_b_ref)
    bottom = own_ref[HALF:QUARTER, :] + decode(bottom_a_ref) + decode(bottom_b_ref)
    for k in range(SPLIT):
        lanes = slice(k * LANES, (k + 1) * LANES)
        out_ref[pl.ds(k, HALF, stride=SPLIT), :] = top[:, lanes]
        out_ref[pl.ds(HALF * SPLIT + k, HALF, stride=SPLIT), :] = bottom[:, lanes]


def finish(own, top_a, top_b, bottom_a, bottom_b):
    return pl.pallas_call(
        finish_kernel,
        out_shape=jax.ShapeDtypeStruct((QUARTER * SPLIT, LANES), F32),
        in_specs=[IN_VMEM] * 5,
        out_specs=IN_VMEM,
        compiler_params=params(4),
    )(own, top_a, top_b, bottom_a, bottom_b)


def shift(value, axis, by):
    n = lax.axis_size(axis)
    return lax.ppermute(value, axis, [(i, (i + by) % n) for i in range(n)])


def to_owners(value):
    return lax.all_to_all(value, ("y", "c"), split_axis=0, concat_axis=0, tiled=True)


def z_ring(left, right):
    up, down = {0: (left, right)}, {0: (left, right)}
    for step in (1, 2, 3):
        up[step] = tuple(shift(v, "z", 1) for v in up[step - 1])
        down[step] = tuple(shift(v, "z", -1) for v in down[step - 1])
    ring = {**up, **{N_Z - step: down[step] for step in (1, 2, 3)}}
    ring[4] = (shift(up[3][0], "z", 1), shift(down[3][1], "z", -1))
    return ring


def on_device(tokens, grads, routing, basis_in, basis_out):
    x, z = lax.axis_index("x"), lax.axis_index("z")
    place = jnp.stack([x ^ 2, (x + 1) & 3, (x + 3) & 3, x]).astype(I32)
    here = z.astype(I32).reshape(1)

    ring = z_ring(*stage(tokens, routing.T))
    packed = pack_grads(here, routing.T, grads.reshape(TOK * TOP, FF), [])
    grads_in = to_owners(packed)
    by_z = regroup(grads_in, [*ring[3], *ring[5]])
    rows_out = [by_z[k] if k == 0 else shift(by_z[k], "z", k) for k in ORDER]

    rows_in = to_owners(
        pack_tokens(here, [ring[k][0] for k in ORDER], [ring[k][1] for k in ORDER], [grads_in])
    )
    g_sq = rotate_grads(rows_out, basis_out)
    a_sq = rotate_inputs(rows_in, basis_in, [g_sq])

    far_up, far_down = far_blocks(place, a_sq, g_sq)
    got_far_up, got_far_down = shift(far_up, "x", 1), shift(far_down, "x", -1)
    near_up, near_down = near_blocks(place, a_sq, g_sq)
    got_near_up, got_near_down = shift(near_up, "x", 1), shift(near_down, "x", -1)
    up, down, own = rest_blocks(place, a_sq, g_sq)
    up, down = pass_on(up, down, got_far_up, got_far_down)
    got_up, got_down = shift(up, "x", 1), shift(down, "x", -1)
    values = finish(own, got_up, got_near_down, got_near_up, got_down)
    return values.reshape(QUARTER, 1, FF)


def solution(mesh):
    split = Mesh(mesh.devices.reshape(N_X, N_Z, N_Y, N_C), ("x", "z", "y", "c"))
    owner = ("z", "y", "c")
    everywhere = ("x", "z", "y", "c")
    return jax.shard_map(
        on_device,
        mesh=split,
        in_specs=(
            P(everywhere, None),
            P(everywhere, None, None),
            P(everywhere, None),
            P(owner, None, None),
            P(owner, None, None),
        ),
        out_specs=P("x", owner, None),
        check_vma=False,
    )
```
